256 devices in a mesh: dp: 16 (over x_hi, z), ctx: 16 (over x_lo, y, core).
Axes of the slice: x: 4 (x_hi: 2, x_lo: 2; x = x_hi * 2 + x_lo), y: 4, z: 8, core: 2. Of those that a mesh axis runs over, the one named last changes fastest.
Arguments:
- events: bfloat16 [65536, 1024], P(('dp', 'ctx')), may hold values from -6 to 6
- w_in: bfloat16 [1024, 4096], replicated, may hold values from -0.1875 to 0.1875
- w_out: bfloat16 [1024, 1024], replicated, may hold values from -0.1875 to 0.1875
- targets: bfloat16 [65536, 1024], P(('dp', 'ctx')), may hold values from -12 to 12
- target_ids: int32 [65536], P(('dp', 'ctx')), may hold values from 0 to 63
- lengths: int32 [16, 4], P('dp'), may hold values from 1 to 2048, 4096 in all within a row
- block_order: int32 [16, 16], P('dp'), may hold values from 0 to 15, each once within a row
- negatives: bfloat16 [2048, 1024], P('dp'), may hold values from -12 to 12
- neg_ids: int32 [2048], replicated, may hold values from 0 to 63
Outputs:
- event_loss: float32 [65536], P(('dp', 'ctx'))
- neg_grad: float32 [2048, 1024], P(('dp', 'ctx'))
The draws below stay inside these ranges and needn't reach their ends.
Inputs may be any that keep to these rules, and one draw needn't show every extreme that they name: `lengths`: each row sums to 4096; its largest entry is exactly 2048. `block_order`: each row holds every number below 16 once.
All inputs are finite; a program needn't handle non-finite values.
Results may differ from the reference program's by a relative error of at most 0.011.
Values may be sent and summed in bfloat16 or wider, within the bound.
A program may use at most 64 MiB of HBM per device.

```python
import math
import jax
import jax.numpy as jnp
import numpy as np
from jax import lax

D = 1024
HEADS = 8
TOK_DEV = 256
NEG_DEV = 128
USERS = 4
ITEMS = 64
TOKENS = 65536
NEG = 2048
N_DP = 16
N_CTX = 16


def draw_events(key, part):
    own_key = jax.random.fold_in(key, 11)
    values = jnp.clip(jax.random.normal(own_key, (TOKENS, D), jnp.float32), -6.0, 6.0)
    return values.astype(jnp.bfloat16)


def draw_targets(key, part):
    own_key = jax.random.fold_in(key, 12)
    values = jnp.clip(2.5 * jax.random.normal(own_key, (TOKENS, D), jnp.float32), -12.0, 12.0)
    return values.astype(jnp.bfloat16)


def draw_negatives(key, part):
    own_key = jax.random.fold_in(key, 13)
    values = jnp.clip(2.5 * jax.random.normal(own_key, (NEG, D), jnp.float32), -12.0, 12.0)
    return values.astype(jnp.bfloat16)


def place_ends(values, rng, least, largest):
    index_at = [jax.random.randint(jax.random.fold_in(rng, axis), (), 0, length) for axis, length in enumerate(values.shape)]
    longest = values.shape.index(max(values.shape))
    beside = index_at[:longest] + [(index_at[longest] + 1) % values.shape[longest]] + index_at[longest + 1:]
    return values.at[tuple(index_at)].set(least).at[tuple(beside)].set(largest)


def split_up(amount, total, most, lean):
    weights = [(1 << 20) // math.isqrt(standing ** lean) + 1 for standing in range(2, amount + 1)]
    spare, given = total - most - (amount - 1), [1] * (amount - 1)
    while spare > 0:
        free = [i for i in range(amount - 1) if given[i] < most]
        whole, left = sum([weights[i] for i in free]), spare
        for i in free:
            addition = min(most - given[i], max(1, left * weights[i] // whole), spare)
            given[i] = given[i] + addition
            spare = spare - addition
    return np.array([most] + given)


def uneven(stream_key, count, total, most, slope):
    if count == 2:
        one = jax.random.randint(stream_key, (), max(1, total - most), min(most, total - 1) + 1)
        return jnp.stack([one, total - one])
    tallies = jnp.asarray(split_up(count, total, most, slope), jnp.int32)
    twos = (count - 1) // 2
    giver, receiver = tallies[1:1 + 2 * twos:2], tallies[2:2 + 2 * twos:2]
    slack = jnp.minimum(giver - 1, most - receiver)
    passed = jax.random.randint(jax.random.fold_in(stream_key, 1), (twos,), 0, 1 << 20) % (slack + 1)
    tallies = tallies.at[1:1 + 2 * twos:2].set(giver - passed).at[2:2 + 2 * twos:2].set(receiver + passed)
    return tallies[jax.random.permutation(jax.random.fold_in(stream_key, 2), count)]


def noise(key, extent, width, bound, kind=jnp.bfloat16):
    return jnp.clip(width * jax.random.normal(key, extent, jnp.float32), -bound, bound).astype(kind)


def setup_inputs(seed: int = 0) -> dict:
    key_of = jax.random.split(jax.random.key(seed), 10)
    events = draw_events(jax.random.fold_in(key_of[9], 71), 0)
    w_in = noise(key_of[1], (D, 4 * D), D ** -0.5, 0.1875)
    w_out = noise(key_of[2], (D, D), D ** -0.5, 0.1875)
    targets = draw_targets(jax.random.fold_in(key_of[9], 71), 0)
    target_ids = place_ends(jax.random.randint(key_of[4], (TOKENS,), 0, ITEMS), jax.random.fold_in(key_of[4], 1), 0, ITEMS - 1).astype(jnp.int32)
    lengths = jax.vmap(lambda own: uneven(own, USERS, TOK_DEV * N_CTX, TOK_DEV * N_CTX // 2, 2))(jax.random.split(key_of[5], N_DP)).reshape((N_DP, USERS)).astype(jnp.int32)
    block_order = jax.vmap(lambda own: jax.random.permutation(own, N_CTX))(jax.random.split(key_of[6], N_DP)).reshape((N_DP, N_CTX)).astype(jnp.int32)
    negatives = draw_negatives(jax.random.fold_in(key_of[9], 71), 0)
    neg_ids = place_ends(jax.random.randint(key_of[8], (NEG,), 0, ITEMS), jax.random.fold_in(key_of[8], 1), 0, ITEMS - 1).astype(jnp.int32)
    return dict(events=events, w_in=w_in, w_out=w_out, targets=targets, target_ids=target_ids, lengths=lengths, block_order=block_order, negatives=negatives, neg_ids=neg_ids)


def layer_norm(values):
    center = values - lax.optimization_barrier(jnp.mean(values, axis=-1, keepdims=True))
    spread = lax.optimization_barrier(jnp.mean(center * center, axis=-1, keepdims=True))
    return center * lax.rsqrt(spread + 1e-05)

def reference(events, w_in, w_out, targets, target_ids, lengths, block_order, negatives, neg_ids):
    seq_rows = TOK_DEV * N_CTX
    head_size = D // HEADS
    scale = 1.0 / math.sqrt(D)

    def group_pass(running_grad, inputs):
        event_rows, target_rows, target_group, user_lens, block_slots = inputs
        normed = layer_norm(event_rows.astype(jnp.float32)).astype(jnp.bfloat16)
        projected = jax.nn.silu(jnp.dot(normed, w_in, preferred_element_type=jnp.float32)).astype(jnp.bfloat16)
        gate_rows = projected[:, :D]
        value_rows = projected[:, D:2 * D]
        query_rows = projected[:, 2 * D:3 * D]
        key_rows = projected[:, 3 * D:]
        positions = (block_slots[:, None] * TOK_DEV + jnp.arange(TOK_DEV, dtype=jnp.int32)[None, :]).reshape(seq_rows)
        user_ends = jnp.cumsum(user_lens)
        user_ids = lax.optimization_barrier(jnp.sum((positions[:, None] >= user_ends[None, :]).astype(jnp.int32), axis=1))
        user_size = lax.optimization_barrier(jnp.sum(jnp.where(user_ids[:, None] == jnp.arange(USERS, dtype=jnp.int32)[None, :], user_lens[None, :], 0), axis=1)).astype(jnp.float32)
        visible = (user_ids[:, None] == user_ids[None, :]) & (positions[None, :] <= positions[:, None])
        outputs = []
        for head_index in range(HEADS):
            head_cols = slice(head_index * head_size, (head_index + 1) * head_size)
            scores = jnp.dot(query_rows[:, head_cols], key_rows[:, head_cols].T, preferred_element_type=jnp.float32) / math.sqrt(head_size)
            weights = (jnp.where(visible, jax.nn.silu(scores), 0.0) / user_size[:, None]).astype(jnp.bfloat16)
            outputs.append(jnp.dot(weights, value_rows[:, head_cols], preferred_element_type=jnp.float32))
        attended = jnp.concatenate(outputs, axis=1)
        mixed = (layer_norm(attended) * gate_rows.astype(jnp.float32)).astype(jnp.bfloat16)
        user_vec = (event_rows.astype(jnp.float32) + jnp.dot(mixed, w_out, preferred_element_type=jnp.float32)).astype(jnp.bfloat16)
        pos_logit = lax.optimization_barrier(jnp.sum(user_vec.astype(jnp.float32) * target_rows.astype(jnp.float32), axis=-1)) * scale
        logits = jnp.dot(user_vec, negatives.T, preferred_element_type=jnp.float32) * scale
        allowed = target_group[:, None] != neg_ids[None, :]
        row_top = jnp.maximum(pos_logit, lax.optimization_barrier(jnp.max(jnp.where(allowed, logits, pos_logit[:, None]), axis=1)))
        denominator = jnp.exp(pos_logit - row_top) + lax.optimization_barrier(jnp.sum(jnp.where(allowed, jnp.exp(logits - row_top[:, None]), 0.0), axis=1))
        log_total = row_top + jnp.log(denominator)
        event_loss = log_total - pos_logit
        sample_prob = jnp.where(allowed, jnp.exp(logits - log_total[:, None]), 0.0).astype(jnp.bfloat16)
        running_grad = running_grad + jnp.dot(sample_prob.T, user_vec, preferred_element_type=jnp.float32) * scale
        return (running_grad, event_loss)
    start_grad = jnp.zeros((NEG_DEV * N_DP, D), jnp.float32)
    neg_grad, losses = lax.scan(group_pass, start_grad, (events.reshape(N_DP, seq_rows, D), targets.reshape(N_DP, seq_rows, D), target_ids.reshape(N_DP, seq_rows), lengths, block_order))
    return (losses.reshape(N_DP * seq_rows), neg_grad)
```

```python
import functools
import math

import jax
import jax.numpy as jnp
from jax import lax
from jax.experimental import pallas as pl
from jax.experimental.pallas import tpu as pltpu
from jax.sharding import PartitionSpec as P

MESH = pl.DeviceIdType.MESH
F32 = jnp.float32
BF16 = jnp.bfloat16
ROWS, WIDTH, HEADS, HEAD = 256, 1024, 8, 128
SLOTS = 16
VMEM_LIMIT = 56 * 2**20


def place():
    dp = lax.axis_index("dp")
    ctx = lax.axis_index("ctx")
    return dp // 8, dp % 8, ctx // 8, (ctx // 2) % 4, ctx % 2


def device(xh, z, xl, y, c):
    return (xh * 8 + z, xl * 8 + y * 2 + c)


def remote(src, dst, send, recv, dev):
    return pltpu.make_async_remote_copy(
        src_ref=src, dst_ref=dst, send_sem=send, recv_sem=recv, device_id=dev, device_id_type=MESH
    )


def greet(others):
    barrier = pltpu.get_barrier_semaphore()
    for other in others:
        pl.semaphore_signal(barrier, inc=1, device_id=other, device_id_type=MESH)
    return barrier, len(others)


def silu(values):
    half = values * 0.5
    return half + half * jnp.tanh(half)


def norm(values):
    center = values - jnp.mean(values, axis=-1, keepdims=True)
    spread = jnp.mean(center * center, axis=-1, keepdims=True)
    return center * lax.rsqrt(spread + 1e-05)


def project_kernel(
    events, w_in, neg_in, gate_out, kv_all, q_all, neg_all,
    w_buf, normed, kv_st, q_st,
    w_sem, loc_sem, kv_ss, kv_rs, kv_fs, q_ss, q_rs, n_xs, n_ss, n_fs, n_rs,
):
    xh, z, xl, y, c = place()
    dp = lax.axis_index("dp")
    me = lax.axis_index("ctx")
    chip = me // 2
    sib = (dp, chip * 2 + 1 - c)
    z_up, z_down = lax.rem(z + 1, 8), lax.rem(z + 7, 8)
    up, down = device(xh, z_up, xl, y, c), device(xh, z_down, xl, y, c)
    across = device(1 - xh, z, xl, y, c)

    barrier, count = greet(
        [(dp, lax.rem(me + k, SLOTS)) for k in range(1, SLOTS)] + [up, down, across]
    )
    offsets = [3072, 1024, 3584, 1536, 2048, 2560, 0, 512]
    w_copies = [
        pltpu.make_async_copy(w_in.at[:, pl.ds(off, 512)], w_buf.at[i], w_sem.at[i])
        for i, off in enumerate(offsets)
    ]
    for copy in w_copies:
        copy.start()
    local = [
        pltpu.make_async_copy(neg_in.at[pl.ds(64 * k, 64)], neg_all.at[dp * 2 + k], loc_sem.at[k])
        for k in range(2)
    ]
    for copy in local:
        copy.start()
    normed[...] = norm(events[...].astype(F32)).astype(BF16)
    pl.semaphore_wait(barrier, count)

    own_neg = neg_in.at[pl.ds(pl.multiple_of(64 * c, 64), 64)]
    sends = []

    def neg_block(xh_, z_, c_):
        return (xh_ * 8 + z_) * 2 + c_

    def start(copy):
        copy.start()
        sends.append(copy)

    mine = neg_block(xh, z, c)
    start(remote(own_neg, neg_all.at[mine], n_xs, n_rs.at[mine], across))
    start(remote(own_neg, neg_all.at[mine], n_ss.at[0, 0], n_rs.at[mine], up))
    start(remote(own_neg, neg_all.at[mine], n_ss.at[1, 0], n_rs.at[mine], down))

    def block(i):
        w_copies[i].wait()
        return silu(jnp.dot(normed[...], w_buf[i], preferred_element_type=F32)).astype(BF16)

    def kv_send(h):
        return remote(kv_st.at[h], kv_all.at[me], kv_ss.at[h], kv_rs.at[me], (dp, 2 * h + c))

    def q_send(h, core):
        return remote(
            q_st.at[h, pl.ds(128 * core, 128)],
            q_all.at[me],
            q_ss.at[h, core],
            q_rs.at[me],
            (dp, 2 * h + core),
        )

    for half in range(2):
        for part in range(2):
            value = block(2 * half + part)
            for k in range(4):
                kv_st[4 * half + k, part] = value[:, 128 * k : 128 * (k + 1)]
        for k in range(4):
            h = 4 * half + k

            @pl.when(h != chip)
            def _(h=h):
                kv_send(h).start()

    kv_sib = remote(kv_st.at[chip], kv_all.at[me], kv_fs.at[me], kv_rs.at[me], sib)
    kv_sib.start()
    kv_own = pltpu.make_async_copy(kv_st.at[chip], kv_all.at[me], loc_sem.at[2])
    kv_own.start()
    for half in range(2):
        value = block(4 + half)
        for k in range(4):
            q_st[4 * half + k] = value[:, 128 * k : 128 * (k + 1)]
        for k in range(4):
            h = 4 * half + k

            @pl.when(h != chip)
            def _(h=h):
                q_send(h, 0).start()
                q_send(h, 1).start()

    rows_mine = pl.ds(pl.multiple_of(128 * c, 128), 128)
    rows_sib = pl.ds(pl.multiple_of(128 * (1 - c), 128), 128)
    q_sib = remote(q_st.at[chip, rows_sib], q_all.at[me], q_ss.at[8, 0], q_rs.at[me], sib)
    q_sib.start()
    q_own = pltpu.make_async_copy(q_st.at[chip, rows_mine], q_all.at[me], loc_sem.at[3])
    q_own.start()
    for half in range(2):
        gate_out[:, pl.ds(512 * half, 512)] = block(6 + half)

    def neg_arrived(index):
        remote(neg_all.at[index], neg_all.at[index], n_xs, n_rs.at[index], sib).wait_recv()

    def neg_pass(index, direction, count):
        target = up if direction == 0 else down
        start(remote(neg_all.at[index], neg_all.at[index], n_ss.at[direction, count], n_rs.at[index], target))

    def neg_sib(index):
        start(remote(neg_all.at[index], neg_all.at[index], n_fs.at[index // 2], n_rs.at[index], sib))

    index = neg_block(1 - xh, z, c)
    neg_arrived(index)
    neg_pass(index, 0, 1)
    neg_pass(index, 1, 1)
    neg_sib(index)
    for s in range(1, 5):
        for xh_ in range(2):
            if s < 4 or xh_ == 0:
                index = neg_block(xh_, lax.rem(z + 8 - s, 8), c)
                neg_arrived(index)
                if s < 3 or (s == 3 and xh_ == 0):
                    neg_pass(index, 0, 2 * s + xh_)
                neg_sib(index)
            if s < 4 or xh_ == 1:
                index = neg_block(xh_, lax.rem(z + s, 8), c)
                neg_arrived(index)
                if s < 3 or (s == 3 and xh_ == 1):
                    neg_pass(index, 1, 2 * s + xh_)
                neg_sib(index)
        if s == 3:
            for k in range(1, 8):
                src = lax.rem(chip + k, 8) * 2 + c
                ref = kv_all.at[src]
                remote(ref, ref, kv_fs.at[src], kv_rs.at[src], sib).wait_recv()
                start(remote(ref, ref, kv_fs.at[src], kv_rs.at[src], sib))

    for k in range(8):
        src = lax.rem(chip + k, 8) * 2 + 1 - c
        ref = kv_all.at[src]
        remote(ref, ref, kv_fs.at[src], kv_rs.at[src], sib).wait_recv()
    for k in range(1, SLOTS):
        src = lax.rem(me + k, SLOTS)
        remote(q_all.at[src], q_all.at[src], q_ss.at[0, 0], q_rs.at[src], sib).wait_recv()
    for xh_ in range(2):
        for k in range(8):
            z_ = lax.rem(z + k, 8)
            index = neg_block(xh_, z_, 1 - c)
            if k > 0:
                neg_arrived(index)
            else:

                @pl.when(xh_ != xh)
                def _(index=index):
                    neg_arrived(index)

    for copy in local + [kv_own, q_own]:
        copy.wait()
    for copy in sends + [kv_sib, q_sib]:
        copy.wait_send()
    for h in range(8):

        @pl.when(h != chip)
        def _(h=h):
            kv_send(h).wait_send()
            q_send(h, 0).wait_send()
            q_send(h, 1).wait_send()


def attend_kernel(lens, order, q, kv, out, slot_of):
    c = lax.axis_index("ctx") % 2
    for s in range(SLOTS):
        slot_of[order[0, s]] = s
    sizes = [lens[0, u] for u in range(4)]
    starts = [0, sizes[0], sizes[0] + sizes[1], sizes[0] + sizes[1] + sizes[2]]

    def pick(pos, values):
        got = jnp.where(pos >= starts[1], values[1], values[0])
        got = jnp.where(pos >= starts[2], values[2], got)
        return jnp.where(pos >= starts[3], values[3], got)

    row = lax.broadcasted_iota(jnp.int32, (ROWS, 1), 0)
    row = jnp.where(row < 128, row, row + 128) + 128 * c
    col = lax.broadcasted_iota(jnp.int32, (1, ROWS), 1)
    factor = 0.5 / math.sqrt(HEAD)

    def pair(p, carry):
        s0, s1 = slot_of[2 * p], slot_of[2 * p + 1]
        query = jnp.concatenate([q[s0], q[s1]], axis=0)
        q_pos = row + 512 * p
        q_start = pick(q_pos, starts)
        q_size = pick(q_pos, sizes).astype(F32)
        first = pick(512 * p + 128 * c, starts) // ROWS

        def step(kb, total):
            s = slot_of[kb]
            scores = lax.dot_general(
                query, kv[s, 0], (((1,), (1,)), ((), ())), preferred_element_type=F32
            )
            half = scores * factor
            weight = half + half * jnp.tanh(half)
            k_pos = col + kb * ROWS
            seen = (k_pos >= q_start) & (k_pos <= q_pos)
            weight = jnp.where(seen, weight, 0.0).astype(BF16)
            return total + jnp.dot(weight, kv[s, 1], preferred_element_type=F32)

        total = lax.fori_loop(first, 2 * p + 2, step, jnp.zeros((ROWS, HEAD), F32))
        total = (total / q_size).astype(BF16)
        out[s0] = total[:128]
        out[s1] = total[128:]
        return carry

    lax.fori_loop(0, SLOTS // 2, pair, 0)


def loss_kernel(
    att, gate_in, events_in, targets_in, target_ids, w_out_in, neg_in, neg_ids,
    loss_out, grad_out,
    heads, gate, events, targets, w_out, neg, mixed, user, user_sib, logits,
    p_own, p_send, p_recv, grad, ra1, rb1, sa, sb, ra2, rb2, tz, rz,
    loc_sem, a_ss, a_rs, u_sem, p_ss, p_rs, g_ss, g_rs, h_ss, h_rs, z_ss, z_rs,
):
    xh, z, xl, y, c = place()
    dp = lax.axis_index("dp")
    me = lax.axis_index("ctx")
    chip = me // 2
    sib = (dp, chip * 2 + 1 - c)
    xs = [(xh, 1 - xl), (1 - xh, xl), (1 - xh, 1 - xl)]
    x_peers = [device(a, z, b, y, c) for a, b in xs]
    ys = [lax.rem(y + k, 4) for k in range(1, 4)]
    y_peers = [device(xh, z, xl, b, c) for b in ys]
    zs = [lax.rem(z + k, 8) for k in range(1, 8)]
    z_peers = [device(xh, b, xl, y, c) for b in zs]

    barrier, count = greet(
        [(dp, lax.rem(me + k, SLOTS)) for k in range(1, SLOTS)] + x_peers[1:] + z_peers
    )
    loads = [
        pltpu.make_async_copy(src, dst, loc_sem.at[i])
        for i, (src, dst) in enumerate(
            [(gate_in, gate), (w_out_in, w_out), (events_in, events), (targets_in, targets), (neg_in, neg)]
        )
    ]
    for copy in loads:
        copy.start()
    pl.semaphore_wait(barrier, count)

    sends = []

    def start(copy):
        copy.start()
        sends.append(copy)

    for k in range(1, SLOTS):
        j = lax.rem(me + k, SLOTS)
        start(remote(att.at[j], heads.at[me], a_ss.at[k], a_rs.at[me], (dp, j)))
    heads[me] = att[me]

    ids = neg_ids[...].astype(F32)
    ids = jnp.concatenate([ids, jnp.zeros((112, 128), F32)], axis=0).T
    wanted = target_ids[...].astype(F32)

    for k in range(1, SLOTS):
        j = lax.rem(me + k, SLOTS)
        remote(heads.at[j], heads.at[j], a_ss.at[0], a_rs.at[j], sib).wait_recv()
    loads[0].wait()
    for core in range(2):
        rows = pl.ds(128 * core, 128)
        attended = jnp.concatenate([heads[2 * h + core] for h in range(HEADS)], axis=1)
        mixed[rows] = (norm(attended.astype(F32)) * gate[rows].astype(F32)).astype(BF16)
    for copy in loads[1:4]:
        copy.wait()
    vec = events[...].astype(F32) + jnp.dot(mixed[...], w_out[...], preferred_element_type=F32)
    user[...] = vec.astype(BF16)
    u_copy = remote(user, user_sib, u_sem.at[0], u_sem.at[1], sib)
    start(u_copy)
    scale = 1.0 / math.sqrt(WIDTH)
    pos_col = jnp.sum(user[...].astype(F32) * targets[...].astype(F32), axis=1, keepdims=True) * scale
    eye = lax.broadcasted_iota(jnp.int32, (ROWS, ROWS), 0) == lax.broadcasted_iota(
        jnp.int32, (ROWS, ROWS), 1
    )
    pos = jnp.sum(jnp.where(eye, pos_col, 0.0), axis=0, keepdims=True)

    loads[4].wait()
    top = pos
    for d in range(SLOTS):
        part = neg[pl.ds(2 * d, 2)].reshape(128, WIDTH)
        scores = (
            lax.dot_general(part, user[...], (((1,), (1,)), ((), ())), preferred_element_type=F32)
            * scale
        )
        allowed = ids[:, d : d + 1] != wanted
        scores = jnp.where(allowed, scores, -jnp.inf)
        top = jnp.maximum(top, jnp.max(scores, axis=0, keepdims=True))
        logits[d] = scores.reshape(8, 2, 8, ROWS)
    total = jnp.exp(pos - top)
    for d in range(SLOTS):
        weight = jnp.exp(logits[d] - top.reshape(1, 1, 1, ROWS))
        logits[d] = weight
        total = total + jnp.sum(weight.reshape(128, ROWS), axis=0, keepdims=True)
    loss_out[...] = top + jnp.log(total) - pos
    inverse = 1.0 / total
    for d in range(SLOTS):
        p_send[pl.ds(64 * d, 64)] = (logits[d, :, 1 - c].reshape(64, ROWS) * inverse).astype(BF16)
    p_copy = remote(p_send, p_recv, p_ss, p_rs, sib)
    start(p_copy)
    for d in range(SLOTS):
        p_own[pl.ds(64 * d, 64)] = (logits[d, :, c].reshape(64, ROWS) * inverse).astype(BF16)
    u_copy.wait_recv()
    p_copy.wait_recv()

    def grad_block(a, b):
        rows = pl.ds(pl.multiple_of((a * 8 + 4 * b) * 64, 256), 256)
        value = jnp.dot(p_own[rows], user[...], preferred_element_type=F32)
        value = value + jnp.dot(p_recv[rows], user_sib[...], preferred_element_type=F32)
        left = value[:, :512].reshape(4, 2, 4, 8, 512)
        right = value[:, 512:].reshape(4, 2, 4, 8, 512)
        grad[a, pl.ds(4 * b, 4)] = jnp.concatenate([left, right], axis=3).astype(BF16)

    def send_x(k):
        a, b = xs[k]
        start(remote(grad.at[a, pl.ds(0, 4), b], ra1.at[k], g_ss.at[k], g_rs.at[k], x_peers[k]))

    def send_y(k, a):
        start(
            remote(
                grad.at[a, pl.ds(4, 4), :, ys[k]],
                rb1.at[k, a],
                g_ss.at[3 + 2 * k + a],
                g_rs.at[3 + 2 * k + a],
                y_peers[k],
            )
        )

    grad_block(1 - xh, 0)
    send_x(1)
    send_x(2)
    grad_block(0, 1)
    for k in range(3):
        send_y(k, 0)
    grad_block(1, 1)
    for k in range(3):
        send_y(k, 1)
    grad_block(xh, 0)
    send_x(0)

    def up(ref):
        return ref[...].astype(F32)

    for k in range(3):
        remote(ra1.at[k], ra1.at[k], g_ss.at[k], g_rs.at[k], sib).wait_recv()
    sa[...] = (
        up(grad.at[xh, pl.ds(0, 4), xl]) + up(ra1.at[0]) + up(ra1.at[1]) + up(ra1.at[2])
    ).astype(BF16)
    for k in range(3):
        start(remote(sa.at[:, ys[k]], ra2.at[k], h_ss.at[k], h_rs.at[k], y_peers[k]))
    for k in range(3):
        for a in range(2):
            ref = rb1.at[k, a]
            remote(ref, ref, g_ss.at[0], g_rs.at[3 + 2 * k + a], sib).wait_recv()
    sb[...] = (
        up(grad.at[:, pl.ds(4, 4), :, y]) + up(rb1.at[0]) + up(rb1.at[1]) + up(rb1.at[2])
    ).astype(BF16)
    for k in range(3):
        a, b = xs[k]
        start(remote(sb.at[a, :, b], rb2.at[k], h_ss.at[3 + k], h_rs.at[3 + k], x_peers[k]))
    for k in range(3):
        remote(ra2.at[k], ra2.at[k], h_ss.at[0], h_rs.at[k], sib).wait_recv()
    tz[pl.ds(0, 4)] = (
        up(sa.at[:, y]) + up(ra2.at[0]) + up(ra2.at[1]) + up(ra2.at[2])
    ).astype(BF16)
    for k in range(3):
        remote(rb2.at[k], rb2.at[k], h_ss.at[0], h_rs.at[3 + k], sib).wait_recv()
    tz[pl.ds(4, 4)] = (
        up(sb.at[xh, :, xl]) + up(rb2.at[0]) + up(rb2.at[1]) + up(rb2.at[2])
    ).astype(BF16)
    for k in range(7):
        start(remote(tz.at[zs[k]], rz.at[k], z_ss.at[k], z_rs.at[k], z_peers[k]))
    for k in range(7):
        remote(rz.at[k], rz.at[k], z_ss.at[0], z_rs.at[k], sib).wait_recv()
    result = tz[z].astype(F32)
    for k in range(7):
        result = result + rz[k].astype(F32)
    result = result * scale
    grad_out[:, :512] = result[:8]
    grad_out[:, 512:] = result[8:]
    for copy in sends:
        copy.wait_send()


def shards(events, w_in, w_out, targets, target_ids, lengths, block_order, negatives, neg_ids):
    any_space = pl.BlockSpec(memory_space=pl.ANY)
    vmem = pl.BlockSpec(memory_space=pltpu.VMEM)
    smem = pl.BlockSpec(memory_space=pltpu.SMEM)
    dma = pltpu.SemaphoreType.DMA
    gate, kv_all, q_all, neg_all = pl.pallas_call(
        project_kernel,
        out_shape=(
            jax.ShapeDtypeStruct((ROWS, WIDTH), BF16),
            jax.ShapeDtypeStruct((SLOTS, 2, ROWS, HEAD), BF16),
            jax.ShapeDtypeStruct((SLOTS, 128, HEAD), BF16),
            jax.ShapeDtypeStruct((32, 64, WIDTH), BF16),
        ),
        in_specs=[vmem, any_space, any_space],
        out_specs=(vmem, any_space, any_space, any_space),
        scratch_shapes=[
            pltpu.VMEM((8, WIDTH, 512), BF16),
            pltpu.VMEM((ROWS, WIDTH), BF16),
            pltpu.VMEM((HEADS, 2, ROWS, HEAD), BF16),
            pltpu.VMEM((HEADS, ROWS, HEAD), BF16),
            dma((8,)),
            dma((4,)),
            dma((8,)),
            dma((SLOTS,)),
            dma((SLOTS,)),
            dma((9, 2)),
            dma((SLOTS,)),
            dma,
            dma((2, 8)),
            dma((SLOTS,)),
            dma((32,)),
        ],
        compiler_params=pltpu.CompilerParams(
            collective_id=1, has_side_effects=True, vmem_limit_bytes=VMEM_LIMIT
        ),
        name="project",
    )(events, w_in, negatives)

    att = pl.pallas_call(
        attend_kernel,
        out_shape=jax.ShapeDtypeStruct((SLOTS, 128, HEAD), BF16),
        in_specs=[smem, smem, vmem, vmem],
        out_specs=vmem,
        scratch_shapes=[pltpu.SMEM((SLOTS,), jnp.int32)],
        compiler_params=pltpu.CompilerParams(vmem_limit_bytes=VMEM_LIMIT),
        name="attend",
    )(lengths, block_order, q_all, kv_all)

    loss, grad = pl.pallas_call(
        loss_kernel,
        out_shape=(
            jax.ShapeDtypeStruct((1, ROWS), F32),
            jax.ShapeDtypeStruct((8, WIDTH), F32),
        ),
        in_specs=[vmem, any_space, any_space, any_space, vmem, any_space, any_space, vmem],
        out_specs=(vmem, vmem),
        scratch_shapes=[
            pltpu.VMEM((SLOTS, 128, HEAD), BF16),
            pltpu.VMEM((ROWS, WIDTH), BF16),
            pltpu.VMEM((ROWS, WIDTH), BF16),
            pltpu.VMEM((ROWS, WIDTH), BF16),
            pltpu.VMEM((WIDTH, WIDTH), BF16),
            pltpu.VMEM((32, 64, WIDTH), BF16),
            pltpu.VMEM((ROWS, WIDTH), BF16),
            pltpu.VMEM((ROWS, WIDTH), BF16),
            pltpu.VMEM((ROWS, WIDTH), BF16),
            pltpu.VMEM((SLOTS, 8, 2, 8, ROWS), F32),
            pltpu.VMEM((1024, ROWS), BF16),
            pltpu.VMEM((1024, ROWS), BF16),
            pltpu.VMEM((1024, ROWS), BF16),
            pltpu.VMEM((2, 8, 2, 4, 16, 512), BF16),
            pltpu.VMEM((3, 4, 4, 16, 512), BF16),
            pltpu.VMEM((3, 2, 4, 2, 16, 512), BF16),
            pltpu.VMEM((4, 4, 16, 512), BF16),
            pltpu.VMEM((2, 4, 2, 16, 512), BF16),
            pltpu.VMEM((3, 4, 16, 512), BF16),
            pltpu.VMEM((3, 4, 16, 512), BF16),
            pltpu.VMEM((8, 16, 512), BF16),
            pltpu.VMEM((7, 16, 512), BF16),
            dma((5,)),
            dma((SLOTS,)),
            dma((SLOTS,)),
            dma((2,)),
            dma,
            dma,
            dma((9,)),
            dma((9,)),
            dma((6,)),
            dma((6,)),
            dma((7,)),
            dma((7,)),
        ],
        compiler_params=pltpu.CompilerParams(
            collective_id=2, has_side_effects=True, vmem_limit_bytes=VMEM_LIMIT
        ),
        name="loss",
    )(
        att, gate, events, targets, target_ids.reshape(1, ROWS), w_out, neg_all,
        neg_ids.reshape(SLOTS, 128),
    )
    return (loss.reshape(ROWS), grad)


def solution(mesh):
    return jax.shard_map(
        shards,
        mesh=mesh,
        in_specs=(
            P(("dp", "ctx"), None),
            P(),
            P(),
            P(("dp", "ctx"), None),
            P(("dp", "ctx")),
            P("dp", None),
            P("dp", None),
            P("dp", None),
            P(),
        ),
        out_specs=(P(("dp", "ctx")), P(("dp", "ctx"), None)),
        check_vma=False,
    )
```

```python
import functools
import math

import jax
import jax.numpy as jnp
from jax import lax
from jax.experimental import pallas as pl
from jax.experimental.pallas import tpu as pltpu
from jax.sharding import PartitionSpec as P

MESH = pl.DeviceIdType.MESH
F32 = jnp.float32
BF16 = jnp.bfloat16
ROWS, WIDTH, HEADS, HEAD = 256, 1024, 8, 128
SLOTS = 16
VMEM_LIMIT = 56 * 2**20
RING = 2
PEERS = [(1, 2), (0, 2), (1, 1), (1, 3), (0, 1), (0, 3), (1, 0)]
TILES = 4


def place():
    dp = lax.axis_index("dp")
    ctx = lax.axis_index("ctx")
    return dp // 8, dp % 8, ctx // 8, (ctx // 2) % 4, ctx % 2


def device(xh, z, xl, y, c):
    return (xh * 8 + z, xl * 8 + y * 2 + c)


def remote(src, dst, send, recv, dev):
    return pltpu.make_async_remote_copy(
        src_ref=src, dst_ref=dst, send_sem=send, recv_sem=recv, device_id=dev, device_id_type=MESH
    )


def greet(others):
    barrier = pltpu.get_barrier_semaphore()
    for other in others:
        pl.semaphore_signal(barrier, inc=1, device_id=other, device_id_type=MESH)
    return barrier, len(others)


def silu(values):
    half = values * 0.5
    return half + half * jnp.tanh(half)


def norm(values):
    center = values - jnp.mean(values, axis=-1, keepdims=True)
    spread = jnp.mean(center * center, axis=-1, keepdims=True)
    return center * lax.rsqrt(spread + 1e-05)


def head_of(xl, y, peer):
    return (xl + peer[0]) % 2 * 4 + lax.rem(y + peer[1], 4)


def ring_blocks(xh, z, s):
    ups = [a * 8 + lax.rem(z + 8 - s, 8) for a in (xh, 1 - xh)]
    downs = [a * 8 + lax.rem(z + s, 8) for a in (xh, 1 - xh)]
    return ups, downs


def project_kernel(
    events, w_in, neg_in, gate_out, kv_all, q_all, neg_all,
    w_buf, normed, kv_st, q_st, neg_rows, neg_st,
    w_sem, loc_sem, kv_ss, kv_rs, kv_fs, q_ss, q_rs, n_xs, n_ss, n_rs,
):
    xh, z, xl, y, c = place()
    dp = lax.axis_index("dp")
    me = lax.axis_index("ctx")
    chip = me // 2
    sib = (dp, chip * 2 + 1 - c)
    z_up, z_down = lax.rem(z + 1, 8), lax.rem(z + 7, 8)
    up, down = device(xh, z_up, xl, y, c), device(xh, z_down, xl, y, c)
    across = device(1 - xh, z, xl, y, c)

    barrier, count = greet(
        [across, up, down] + [(dp, lax.rem(me + k, SLOTS)) for k in range(1, SLOTS)]
    )
    far = (1 - xl) * 512
    near = xl * 512
    offsets = [3072 + far, 1024 + far, 3072 + near, 1024 + near, 2048, 2560, 0, 512]
    w_copies = [
        pltpu.make_async_copy(
            w_in.at[:, pl.ds(pl.multiple_of(off, 512), 512)], w_buf.at[i], w_sem.at[i]
        )
        for i, off in enumerate(offsets)
    ]
    for copy in w_copies:
        copy.start()
    neg_rows[...] = neg_in[...].astype(F32).reshape(8, 2, 8, WIDTH)
    neg_st[...] = neg_rows[:, c].reshape(64, WIDTH).astype(BF16)
    neg_own = pltpu.make_async_copy(neg_st, neg_all.at[dp], loc_sem.at[0])
    neg_own.start()
    normed[...] = norm(events[...].astype(F32)).astype(BF16)
    pl.semaphore_wait(barrier, count)

    sends = []

    def start(copy):
        copy.start()
        sends.append(copy)

    start(remote(neg_st, neg_all.at[dp], n_xs, n_rs.at[dp], across))
    start(remote(neg_st, neg_all.at[dp], n_ss.at[0, 0], n_rs.at[dp], up))
    start(remote(neg_st, neg_all.at[dp], n_ss.at[1, 0], n_rs.at[dp], down))

    def ring(s, side):
        ups, downs = ring_blocks(xh, z, s)
        for direction, index in enumerate([ups[side], downs[side]]):
            if s == 0 and direction == 1:
                continue
            ref = neg_all.at[index]
            remote(ref, ref, n_xs, n_rs.at[index], sib).wait_recv()
        if s < RING:
            for direction, index in enumerate([ups[side], downs[side]]):
                ref = neg_all.at[index]
                target = up if direction == 0 else down
                start(remote(ref, ref, n_ss.at[direction, 2 * s + side], n_rs.at[index], target))

    def block(i):
        w_copies[i].wait()
        return silu(jnp.dot(normed[...], w_buf[i], preferred_element_type=F32)).astype(BF16)

    def kv_send(i):
        h = head_of(xl, y, PEERS[i])
        start(remote(kv_st.at[h], kv_all.at[me], kv_ss.at[i], kv_rs.at[me], (dp, 2 * h + c)))

    def q_send(i):
        h = head_of(xl, y, PEERS[i])
        for core in range(2):
            part = q_st.at[h, pl.ds(128 * core, 128)]
            start(remote(part, q_all.at[me], q_ss.at[i, core], q_rs.at[me], (dp, 2 * h + core)))

    for half, side in enumerate([1 - xl, xl]):
        for part in range(2):
            value = block(2 * half + part)
            for k in range(4):
                kv_st[4 * side + k, part] = value[:, 128 * k : 128 * (k + 1)]
        for i in range(7):
            if PEERS[i][0] == 1 - half:
                kv_send(i)
    ring(1, 0)
    kv_sib = remote(kv_st.at[chip], kv_all.at[me], kv_fs.at[me], kv_rs.at[me], sib)
    kv_sib.start()
    kv_own = pltpu.make_async_copy(kv_st.at[chip], kv_all.at[me], loc_sem.at[1])
    kv_own.start()
    for half in range(2):
        value = block(4 + half)
        for k in range(4):
            q_st[4 * half + k] = value[:, 128 * k : 128 * (k + 1)]
    ring(0, 1)
    for i in range(7):
        q_send(i)

    rows_mine = pl.ds(pl.multiple_of(128 * c, 128), 128)
    rows_sib = pl.ds(pl.multiple_of(128 * (1 - c), 128), 128)
    q_sib = remote(q_st.at[chip, rows_sib], q_all.at[me], q_ss.at[7, 0], q_rs.at[me], sib)
    q_sib.start()
    q_own = pltpu.make_async_copy(q_st.at[chip, rows_mine], q_all.at[me], loc_sem.at[2])
    q_own.start()
    gate_out[:, pl.ds(0, 512)] = block(6)
    gate_out[:, pl.ds(512, 512)] = block(7)
    ring(1, 1)
    for s in range(2, RING + 1):
        ring(s, 0)
        ring(s, 1)

    for i in range(7):
        src = head_of(xl, y, PEERS[i]) * 2 + c
        ref = kv_all.at[src]
        remote(ref, ref, kv_fs.at[src], kv_rs.at[src], sib).wait_recv()
        start(remote(ref, ref, kv_fs.at[src], kv_rs.at[src], sib))
    for k in range(1, SLOTS):
        src = lax.rem(me + k, SLOTS)
        remote(q_all.at[src], q_all.at[src], q_ss.at[0, 0], q_rs.at[src], sib).wait_recv()
    for k in range(8):
        src = lax.rem(chip + k, 8) * 2 + 1 - c
        ref = kv_all.at[src]
        remote(ref, ref, kv_fs.at[src], kv_rs.at[src], sib).wait_recv()
    for copy in [neg_own, kv_own, q_own]:
        copy.wait()
    for copy in sends + [kv_sib, q_sib]:
        copy.wait_send()


def attend_kernel(lens, order, q, kv, out, slot_of, work, total, q_start, query, key):
    c = lax.axis_index("ctx") % 2
    for s in range(SLOTS):
        slot_of[order[0, s]] = s
    sizes = [lens[0, u] for u in range(4)]
    starts = [0, sizes[0], sizes[0] + sizes[1], sizes[0] + sizes[1] + sizes[2]]

    def pick(pos, values):
        got = jnp.where(pos >= starts[1], values[1], values[0])
        got = jnp.where(pos >= starts[2], values[2], got)
        return jnp.where(pos >= starts[3], values[3], got)

    row = lax.broadcasted_iota(jnp.int32, (ROWS, HEAD), 0)
    row = jnp.where(row < 128, row, row + 128) + 128 * c
    col = lax.broadcasted_iota(jnp.int32, (ROWS, HEAD), 1)
    factor = 0.5 / math.sqrt(HEAD)

    count = 0
    for p in range(SLOTS // 2):

        def put(kb, n, p=p):
            work[n] = p * SLOTS + kb
            return n + 1

        first = pick(512 * p + 128 * c, starts) // ROWS
        count = lax.fori_loop(first, 2 * p + 2, put, count)
    for u in range(TILES):
        work[count + u] = SLOTS - 1

    for p in range(SLOTS // 2):
        q_start[p] = pick(row + 512 * p, starts)
        query[p, :128] = q[slot_of[2 * p]]
        query[p, 128:] = q[slot_of[2 * p + 1]]
    for s in range(SLOTS):
        key[s] = kv[s, 0].T
    total[...] = jnp.zeros_like(total)

    def step(i, carry):
        found = []
        for u in range(TILES):
            item = work[TILES * i + u]
            p, kb = item // SLOTS, item % SLOTS
            s = slot_of[kb]
            half = jnp.dot(query[p], key[s], preferred_element_type=F32) * factor
            weight = half + half * jnp.tanh(half)
            q_pos = row + 512 * p
            low = q_start[p]
            parts = []
            for j in range(2):
                k_pos = col + (kb * ROWS + HEAD * j)
                seen = (k_pos >= low) & (k_pos <= q_pos)
                part = weight[:, HEAD * j : HEAD * (j + 1)]
                parts.append(jnp.where(seen, part, 0.0).astype(BF16))
            weight = jnp.concatenate(parts, axis=1)
            found.append((p, jnp.dot(weight, kv[s, 1], preferred_element_type=F32)))
        for p, value in found:
            total[p] += value
        return carry

    lax.fori_loop(0, (count + TILES - 1) // TILES, step, 0)
    for p in range(SLOTS // 2):
        size = pick(row + 512 * p, sizes).astype(F32)
        value = (total[p] / size).astype(BF16)
        out[slot_of[2 * p]] = value[:128]
        out[slot_of[2 * p + 1]] = value[128:]


def loss_kernel(
    att, gate_in, events_in, targets_in, target_ids, w_out_in, neg_in, neg_ids,
    loss_out, grad_out,
    heads, gate, events, targets, w_out, neg, mixed, users, wanted, stats, stats_sib,
    logits, prob, grad, ra1, rb1, sa, sb, ra2, rb2, tz, rz,
    loc_sem, neg_sem, n_ss, n_rs, a_ss, a_rs, u_sem, t_sem, s_sem,
    g_ss, g_rs, h_ss, h_rs, z_ss, z_rs,
):
    xh, z, xl, y, c = place()
    dp = lax.axis_index("dp")
    me = lax.axis_index("ctx")
    chip = me // 2
    sib = (dp, chip * 2 + 1 - c)
    xs = [(xh, 1 - xl), (1 - xh, xl), (1 - xh, 1 - xl)]
    x_peers = [device(a, z, b, y, c) for a, b in xs]
    ys = [lax.rem(y + k, 4) for k in range(1, 4)]
    y_peers = [device(xh, z, xl, b, c) for b in ys]
    zs = [lax.rem(z + k, 8) for k in range(1, 8)]
    z_peers = [device(xh, b, xl, y, c) for b in zs]

    barrier, count = greet(
        [(dp, lax.rem(me + k, SLOTS)) for k in range(1, SLOTS)] + z_peers + x_peers[1:]
    )
    loads = [
        pltpu.make_async_copy(src, dst, loc_sem.at[i])
        for i, (src, dst) in enumerate(
            [(gate_in, gate), (w_out_in, w_out), (events_in, events), (targets_in, targets)]
        )
    ]
    held = [xh * 8 + z, (1 - xh) * 8 + z]
    for s in range(1, RING + 1):
        ups, downs = ring_blocks(xh, z, s)
        held += ups + downs
    loads += [
        pltpu.make_async_copy(neg_in.at[index], neg.at[index], neg_sem.at[i])
        for i, index in enumerate(held)
    ]
    for copy in loads:
        copy.start()
    pl.semaphore_wait(barrier, count)

    sends = []

    def start(copy):
        copy.start()
        sends.append(copy)

    def ring_send(source, index, direction, i):
        target = z_peers[0] if direction == 0 else z_peers[6]
        start(remote(source, neg.at[index], n_ss.at[direction, i], n_rs.at[index], target))

    def ring_wait(index):
        remote(neg.at[index], neg.at[index], n_ss.at[0, 0], n_rs.at[index], sib).wait_recv()

    ups = [lax.rem(z + 8 - s, 8) for s in range(5)]
    downs = [lax.rem(z + s, 8) for s in range(5)]
    if RING == 2:
        for i in range(2):
            index = 8 * i + ups[2]
            ring_send(neg_in.at[index], index, 0, i)
            index = 8 * i + downs[2]
            ring_send(neg_in.at[index], index, 1, i)
    else:
        ring_send(neg_in.at[ups[3]], ups[3], 0, 0)
        ring_send(neg_in.at[8 + downs[3]], 8 + downs[3], 1, 0)

    for i in range(7):
        h = head_of(xl, y, PEERS[i])
        for core in range(2):
            j = 2 * h + core
            start(remote(att.at[j], heads.at[me], a_ss.at[2 * i + core], a_rs.at[me], (dp, j)))
    start(remote(att.at[chip * 2 + 1 - c], heads.at[me], a_ss.at[14], a_rs.at[me], sib))
    heads[me] = att[me]

    wanted[0] = target_ids[...].astype(F32)
    t_copy = remote(wanted.at[0], wanted.at[1], t_sem.at[0], t_sem.at[1], sib)
    start(t_copy)
    ids = neg_ids[...].astype(F32)
    ids = jnp.concatenate([ids, jnp.zeros((112, 128), F32)], axis=0).T.reshape(8, 2, 8, 128)
    ids = jnp.where(c == 0, ids[:, 0], ids[:, 1]).reshape(64, 128)

    if RING == 2:
        for i in range(2):
            ring_wait(8 * i + ups[3])
            ring_wait(8 * i + downs[3])
        ring_send(neg.at[ups[3]], ups[3], 0, 2)
        ring_send(neg.at[8 + downs[3]], 8 + downs[3], 1, 2)

    for k in range(1, SLOTS):
        j = lax.rem(me + k, SLOTS)
        remote(heads.at[j], heads.at[j], a_ss.at[0], a_rs.at[j], sib).wait_recv()
    loads[0].wait()
    for core in range(2):
        rows = pl.ds(128 * core, 128)
        attended = jnp.concatenate([heads[2 * h + core] for h in range(HEADS)], axis=1)
        mixed[rows] = (norm(attended.astype(F32)) * gate[rows].astype(F32)).astype(BF16)
    for copy in loads[1:4]:
        copy.wait()
    vec = events[...].astype(F32) + jnp.dot(mixed[...], w_out[...], preferred_element_type=F32)
    users[0] = vec.astype(BF16)
    u_copy = remote(users.at[0], users.at[1], u_sem.at[0], u_sem.at[1], sib)
    start(u_copy)
    scale = 1.0 / math.sqrt(WIDTH)
    pos_col = jnp.sum(users[0].astype(F32) * targets[...].astype(F32), axis=1, keepdims=True) * scale
    eye = lax.broadcasted_iota(jnp.int32, (ROWS, ROWS), 0) == lax.broadcasted_iota(
        jnp.int32, (ROWS, ROWS), 1
    )
    pos = jnp.sum(jnp.where(eye, pos_col, 0.0), axis=0, keepdims=True)

    for copy in loads[4:]:
        copy.wait()
    ring_wait(ups[4])
    ring_wait(8 + downs[4])

    def score(side, top):
        for d in range(0, SLOTS, 4):
            part = neg[pl.ds(d, 4)].reshape(ROWS, WIDTH)
            scores = (
                lax.dot_general(
                    part, users[side], (((1,), (1,)), ((), ())), preferred_element_type=F32
                )
                * scale
            )
            id_col = jnp.concatenate([ids[:, d + i : d + i + 1] for i in range(4)], axis=0)
            scores = jnp.where(id_col != wanted[side], scores, -jnp.inf)
            top = jnp.maximum(top, jnp.max(scores, axis=0, keepdims=True))
            logits[side, pl.ds(64 * d, ROWS)] = scores
        return top

    def weigh(side, top, total):
        for d in range(4):
            rows = pl.ds(ROWS * d, ROWS)
            weight = jnp.exp(logits[side, rows] - top)
            logits[side, rows] = weight
            total = total + jnp.sum(weight, axis=0, keepdims=True)
        stats[2 * side : 2 * side + 1] = top
        stats[2 * side + 1 : 2 * side + 2] = total

    top = score(0, pos)
    weigh(0, top, jnp.exp(pos - top))
    t_copy.wait_recv()
    u_copy.wait_recv()
    top = score(1, jnp.full((1, ROWS), -1e30, F32))
    weigh(1, top, jnp.zeros((1, ROWS), F32))
    s_copy = remote(stats, stats_sib, s_sem.at[0], s_sem.at[1], sib)
    start(s_copy)
    s_copy.wait_recv()
    for side in range(2):
        near_top, near_sum = stats[2 * side : 2 * side + 1], stats[2 * side + 1 : 2 * side + 2]
        far = 2 * (1 - side)
        far_top, far_sum = stats_sib[far : far + 1], stats_sib[far + 1 : far + 2]
        top = jnp.maximum(near_top, far_top)
        near, far = jnp.exp(near_top - top), jnp.exp(far_top - top)
        total = near_sum * near + far_sum * far
        if side == 0:
            loss_out[...] = top + jnp.log(total) - pos
        factor = near / total
        for d in range(4):
            rows = pl.ds(ROWS * d, ROWS)
            prob[rows, pl.ds(ROWS * side, ROWS)] = (logits[side, rows] * factor).astype(BF16)

    def grad_block(n, a, b):
        rows = pl.ds(pl.multiple_of((a * 8 + 4 * b) * 64, 256), 256)
        sides = []
        for k in range(2):
            value = jnp.dot(
                prob[rows],
                users[:, :, pl.ds(512 * k + 256 * n, 256)].reshape(2 * ROWS, 256),
                preferred_element_type=F32,
            )
            sides.append(value.reshape(4, 2, 4, 8, 256))
        grad[n, a, pl.ds(4 * b, 4)] = jnp.concatenate(sides, axis=3).astype(BF16)

    def send_x(n, k):
        a, b = xs[k]
        start(
            remote(
                grad.at[n, a, pl.ds(0, 4), b], ra1.at[n, k], g_ss.at[n, k], g_rs.at[n, k], x_peers[k]
            )
        )

    def send_y(n, k, a):
        i = 3 + 2 * k + a
        start(
            remote(
                grad.at[n, a, pl.ds(4, 4), :, ys[k]],
                rb1.at[n, k, a],
                g_ss.at[n, i],
                g_rs.at[n, i],
                y_peers[k],
            )
        )

    for n in range(2):
        grad_block(n, 1 - xh, 0)
        send_x(n, 2)
        send_x(n, 1)
        grad_block(n, 0, 1)
        for k in (1, 0, 2):
            send_y(n, k, 0)
        grad_block(n, xh, 0)
        send_x(n, 0)
        grad_block(n, 1, 1)
        for k in (1, 0, 2):
            send_y(n, k, 1)

    def up(ref):
        return ref[...].astype(F32)

    for n in range(2):
        for k in range(3):
            remote(ra1.at[n, k], ra1.at[n, k], g_ss.at[n, k], g_rs.at[n, k], sib).wait_recv()
        sa[n] = (
            up(grad.at[n, xh, pl.ds(0, 4), xl]) + up(ra1.at[n, 0]) + up(ra1.at[n, 1]) + up(ra1.at[n, 2])
        ).astype(BF16)
        for k in (1, 0, 2):
            start(
                remote(sa.at[n, :, ys[k]], ra2.at[n, k], h_ss.at[n, k], h_rs.at[n, k], y_peers[k])
            )
        for k in range(3):
            for a in range(2):
                ref = rb1.at[n, k, a]
                remote(ref, ref, g_ss.at[n, 0], g_rs.at[n, 3 + 2 * k + a], sib).wait_recv()
        sb[n] = (
            up(grad.at[n, :, pl.ds(4, 4), :, y])
            + up(rb1.at[n, 0])
            + up(rb1.at[n, 1])
            + up(rb1.at[n, 2])
        ).astype(BF16)
        for k in (2, 1, 0):
            a, b = xs[k]
            start(
                remote(
                    sb.at[n, a, :, b], rb2.at[n, k], h_ss.at[n, 3 + k], h_rs.at[n, 3 + k], x_peers[k]
                )
            )
    for n in range(2):
        for k in range(3):
            remote(ra2.at[n, k], ra2.at[n, k], h_ss.at[n, 0], h_rs.at[n, k], sib).wait_recv()
        tz[n, pl.ds(0, 4)] = (
            up(sa.at[n, :, y]) + up(ra2.at[n, 0]) + up(ra2.at[n, 1]) + up(ra2.at[n, 2])
        ).astype(BF16)
        for k in range(3):
            remote(rb2.at[n, k], rb2.at[n, k], h_ss.at[n, 0], h_rs.at[n, 3 + k], sib).wait_recv()
        tz[n, pl.ds(4, 4)] = (
            up(sb.at[n, xh, :, xl]) + up(rb2.at[n, 0]) + up(rb2.at[n, 1]) + up(rb2.at[n, 2])
        ).astype(BF16)
        for k in (3, 2, 4, 1, 5, 0, 6):
            start(remote(tz.at[n, zs[k]], rz.at[n, k], z_ss.at[n, k], z_rs.at[n, k], z_peers[k]))
    for n in range(2):
        result = tz[n, z].astype(F32)
        for k in range(7):
            remote(rz.at[n, k], rz.at[n, k], z_ss.at[n, 0], z_rs.at[n, k], sib).wait_recv()
            result = result + rz[n, k].astype(F32)
        result = result * scale
        grad_out[:, pl.ds(256 * n, 256)] = result[:8]
        grad_out[:, pl.ds(512 + 256 * n, 256)] = result[8:]
    for copy in sends:
        copy.wait_send()


def shards(events, w_in, w_out, targets, target_ids, lengths, block_order, negatives, neg_ids):
    any_space = pl.BlockSpec(memory_space=pl.ANY)
    vmem = pl.BlockSpec(memory_space=pltpu.VMEM)
    smem = pl.BlockSpec(memory_space=pltpu.SMEM)
    dma = pltpu.SemaphoreType.DMA
    gate, kv_all, q_all, neg_all = pl.pallas_call(
        project_kernel,
        out_shape=(
            jax.ShapeDtypeStruct((ROWS, WIDTH), BF16),
            jax.ShapeDtypeStruct((SLOTS, 2, ROWS, HEAD), BF16),
            jax.ShapeDtypeStruct((SLOTS, 128, HEAD), BF16),
            jax.ShapeDtypeStruct((SLOTS, 64, WIDTH), BF16),
        ),
        in_specs=[vmem, any_space, vmem],
        out_specs=(vmem, any_space, any_space, any_space),
        scratch_shapes=[
            pltpu.VMEM((8, WIDTH, 512), BF16),
            pltpu.VMEM((ROWS, WIDTH), BF16),
            pltpu.VMEM((HEADS, 2, ROWS, HEAD), BF16),
            pltpu.VMEM((HEADS, ROWS, HEAD), BF16),
            pltpu.VMEM((8, 2, 8, WIDTH), F32),
            pltpu.VMEM((64, WIDTH), BF16),
            dma((8,)),
            dma((3,)),
            dma((8,)),
            dma((SLOTS,)),
            dma((SLOTS,)),
            dma((8, 2)),
            dma((SLOTS,)),
            dma,
            dma((2, 2 * RING)),
            dma((SLOTS,)),
        ],
        compiler_params=pltpu.CompilerParams(
            collective_id=1, has_side_effects=True, vmem_limit_bytes=VMEM_LIMIT
        ),
        name="project",
    )(events, w_in, negatives)

    att = pl.pallas_call(
        attend_kernel,
        out_shape=jax.ShapeDtypeStruct((SLOTS, 128, HEAD), BF16),
        in_specs=[smem, smem, vmem, vmem],
        out_specs=vmem,
        scratch_shapes=[
            pltpu.SMEM((SLOTS,), jnp.int32),
            pltpu.SMEM((96,), jnp.int32),
            pltpu.VMEM((SLOTS // 2, ROWS, HEAD), F32),
            pltpu.VMEM((SLOTS // 2, ROWS, HEAD), jnp.int32),
            pltpu.VMEM((SLOTS // 2, ROWS, HEAD), BF16),
            pltpu.VMEM((SLOTS, HEAD, ROWS), BF16),
        ],
        compiler_params=pltpu.CompilerParams(vmem_limit_bytes=VMEM_LIMIT),
        name="attend",
    )(lengths, block_order, q_all, kv_all)

    loss, grad = pl.pallas_call(
        loss_kernel,
        out_shape=(
            jax.ShapeDtypeStruct((1, ROWS), F32),
            jax.ShapeDtypeStruct((8, WIDTH), F32),
        ),
        in_specs=[vmem, any_space, any_space, any_space, vmem, any_space, any_space, vmem],
        out_specs=(vmem, vmem),
        scratch_shapes=[
            pltpu.VMEM((SLOTS, 128, HEAD), BF16),
            pltpu.VMEM((ROWS, WIDTH), BF16),
            pltpu.VMEM((ROWS, WIDTH), BF16),
            pltpu.VMEM((ROWS, WIDTH), BF16),
            pltpu.VMEM((WIDTH, WIDTH), BF16),
            pltpu.VMEM((SLOTS, 64, WIDTH), BF16),
            pltpu.VMEM((ROWS, WIDTH), BF16),
            pltpu.VMEM((2, ROWS, WIDTH), BF16),
            pltpu.VMEM((2, 1, ROWS), F32),
            pltpu.VMEM((8, ROWS), F32),
            pltpu.VMEM((8, ROWS), F32),
            pltpu.VMEM((2, 1024, ROWS), F32),
            pltpu.VMEM((1024, 2 * ROWS), BF16),
            pltpu.VMEM((2, 2, 8, 2, 4, 16, 256), BF16),
            pltpu.VMEM((2, 3, 4, 4, 16, 256), BF16),
            pltpu.VMEM((2, 3, 2, 4, 2, 16, 256), BF16),
            pltpu.VMEM((2, 4, 4, 16, 256), BF16),
            pltpu.VMEM((2, 2, 4, 2, 16, 256), BF16),
            pltpu.VMEM((2, 3, 4, 16, 256), BF16),
            pltpu.VMEM((2, 3, 4, 16, 256), BF16),
            pltpu.VMEM((2, 8, 16, 256), BF16),
            pltpu.VMEM((2, 7, 16, 256), BF16),
            dma((4,)),
            dma((2 + 4 * RING,)),
            dma((2, 3)),
            dma((SLOTS,)),
            dma((15,)),
            dma((SLOTS,)),
            dma((2,)),
            dma((2,)),
            dma((2,)),
            dma((2, 9)),
            dma((2, 9)),
            dma((2, 6)),
            dma((2, 6)),
            dma((2, 7)),
            dma((2, 7)),
        ],
        compiler_params=pltpu.CompilerParams(
            collective_id=2, has_side_effects=True, vmem_limit_bytes=VMEM_LIMIT
        ),
        name="loss",
    )(
        att, gate, events, targets, target_ids.reshape(1, ROWS), w_out, neg_all,
        neg_ids.reshape(SLOTS, 128),
    )
    return (loss.reshape(ROWS), grad)


def solution(mesh):
    return jax.shard_map(
        shards,
        mesh=mesh,
        in_specs=(
            P(("dp", "ctx"), None),
            P(),
            P(),
            P(("dp", "ctx"), None),
            P(("dp", "ctx")),
            P("dp", None),
            P("dp", None),
            P("dp", None),
            P(),
        ),
        out_specs=(P(("dp", "ctx")), P(("dp", "ctx"), None)),
        check_vma=False,
    )
```

```python
import functools
import math

import jax
import jax.numpy as jnp
from jax import lax
from jax.experimental import pallas as pl
from jax.experimental.pallas import tpu as pltpu
from jax.sharding import PartitionSpec as P

MESH = pl.DeviceIdType.MESH
F32 = jnp.float32
BF16 = jnp.bfloat16
ROWS, WIDTH, HEADS, HEAD = 256, 1024, 8, 128
SLOTS = 16
VMEM_LIMIT = 56 * 2**20
PEERS = [(1, 0), (0, 1), (1, 1), (0, 3), (1, 3), (0, 2), (1, 2)]


def place():
    dp = lax.axis_index("dp")
    ctx = lax.axis_index("ctx")
    return dp // 8, dp % 8, ctx // 8, (ctx // 2) % 4, ctx % 2


def device(xh, z, xl, y, c):
    return (xh * 8 + z, xl * 8 + y * 2 + c)


def remote(src, dst, send, recv, dev):
    return pltpu.make_async_remote_copy(
        src_ref=src, dst_ref=dst, send_sem=send, recv_sem=recv, device_id=dev, device_id_type=MESH
    )


def greet(others):
    barrier = pltpu.get_barrier_semaphore()
    for other in others:
        pl.semaphore_signal(barrier, inc=1, device_id=other, device_id_type=MESH)
    return barrier, len(others)


def silu(values):
    half = values * 0.5
    return half + half * jnp.tanh(half)


def norm(values):
    center = values - jnp.mean(values, axis=-1, keepdims=True)
    spread = jnp.mean(center * center, axis=-1, keepdims=True)
    return center * lax.rsqrt(spread + 1e-05)


def program_kernel(
    events, w_in, neg_in, lens, order, targets_in, target_ids, w_out_in, neg_ids,
    loss_out, grad_out,
    w_buf, normed, kv_st, q_st, kv_buf, q_buf, key, q_pos, q_low, total, att_st, k_from,
    heads, gate, targets, w_out, neg_rows, neg, mixed, users, wanted, stats, stats_sib,
    logits, prob, grad, ra1, rb1, sa, sb, ra2, rb2, tz, rz,
    w_sem, loc_sem, kv_ss, kv_fs, kv_rs, q_ss, q_rs, n_xs, n_ss, n_rs, a_ss, a_rs,
    u_sem, t_sem, s_sem, g_ss, g_rs, h_ss, h_rs, z_ss, z_rs,
):
    xh, z, xl, y, c = place()
    dp = lax.axis_index("dp")
    me = lax.axis_index("ctx")
    chip = me // 2
    sib = (dp, chip * 2 + 1 - c)
    xs = [(xh, 1 - xl), (1 - xh, xl), (1 - xh, 1 - xl)]
    x_peers = [device(a, z, b, y, c) for a, b in xs]
    ys = [lax.rem(y + k, 4) for k in range(1, 4)]
    y_peers = [device(xh, z, xl, b, c) for b in ys]
    zs = [lax.rem(z + k, 8) for k in range(1, 8)]
    z_peers = [device(xh, b, xl, y, c) for b in zs]
    up, down, across = z_peers[0], z_peers[6], x_peers[1]
    goes = [chip] + [(xl + a) % 2 * 4 + lax.rem(y + b, 4) for a, b in PEERS]
    comes = [chip] + [(xl + a) % 2 * 4 + lax.rem(y + 4 - b, 4) for a, b in PEERS]

    barrier, count = greet(
        x_peers[1:] + z_peers + [(dp, lax.rem(me + k, SLOTS)) for k in range(1, SLOTS)]
    )
    far = (1 - xl) * 512
    near = xl * 512
    offsets = [3072 + far, 1024 + far, 2048 + far, 3072 + near, 1024 + near, 2048 + near, 0, 512]
    w_copies = [
        pltpu.make_async_copy(
            w_in.at[:, pl.ds(pl.multiple_of(off, 512), 512)], w_buf.at[i], w_sem.at[i]
        )
        for i, off in enumerate(offsets)
    ]
    for copy in w_copies:
        copy.start()
    loads = [
        pltpu.make_async_copy(w_out_in, w_out, loc_sem.at[0]),
        pltpu.make_async_copy(targets_in, targets, loc_sem.at[1]),
    ]
    for copy in loads:
        copy.start()
    neg_rows[...] = neg_in[...].astype(F32).reshape(8, 2, 8, WIDTH)
    neg[dp] = neg_rows[:, c].reshape(64, WIDTH).astype(BF16)
    normed[...] = norm(events[...].astype(F32)).astype(BF16)
    wanted[0] = target_ids[...].astype(F32)
    pl.semaphore_wait(barrier, count)

    sends = []

    def start(copy):
        copy.start()
        sends.append(copy)

    start(remote(neg.at[dp], neg.at[dp], n_xs, n_rs.at[dp], across))
    start(remote(neg.at[dp], neg.at[dp], n_ss.at[0, 0], n_rs.at[dp], up))
    start(remote(neg.at[dp], neg.at[dp], n_ss.at[1, 0], n_rs.at[dp], down))
    t_copy = remote(wanted.at[0], wanted.at[1], t_sem.at[0], t_sem.at[1], sib)
    start(t_copy)

    def neg_wait(index):
        remote(neg.at[index], neg.at[index], n_xs, n_rs.at[index], sib).wait_recv()

    def neg_pass(index, direction, i):
        target = up if direction == 0 else down
        start(remote(neg.at[index], neg.at[index], n_ss.at[direction, i], n_rs.at[index], target))

    def ring(s, side):
        mine = xh if side == 0 else 1 - xh
        ups = mine * 8 + lax.rem(z + 8 - s, 8)
        downs = mine * 8 + lax.rem(z + s, 8)
        neg_wait(ups)
        if s > 0:
            neg_wait(downs)
        if s < 3:
            neg_pass(ups, 0, 2 * s + side)
            neg_pass(downs, 1, 2 * s + side)
        elif side == 1:
            neg_pass(lax.rem(z + 5, 8), 0, 6)
            neg_pass(8 + lax.rem(z + 3, 8), 1, 6)

    def block(i):
        w_copies[i].wait()
        return silu(jnp.dot(normed[...], w_buf[i], preferred_element_type=F32)).astype(BF16)

    def kv_send(i):
        h = goes[i]
        start(remote(kv_st.at[h], kv_buf.at[i, :, c], kv_ss.at[i], kv_rs.at[i, c], (dp, 2 * h + c)))

    def q_send(i):
        h = goes[i]
        for core in range(2):
            part = q_st.at[h, pl.ds(128 * core, 128)]
            start(remote(part, q_buf.at[i, c], q_ss.at[i, core], q_rs.at[i, c], (dp, 2 * h + core)))

    def kv_block(i, part, side):
        value = block(i)
        for k in range(4):
            kv_st[4 * side + k, part] = value[:, 128 * k : 128 * (k + 1)]

    def q_block(i, side):
        value = block(i)
        for k in range(4):
            q_st[4 * side + k] = value[:, 128 * k : 128 * (k + 1)]

    kv_block(0, 0, 1 - xl)
    kv_block(1, 1, 1 - xl)
    kv_send(1)
    q_block(2, 1 - xl)
    q_send(1)
    kv_block(3, 0, xl)
    kv_block(4, 1, xl)
    kv_send(2)
    start(remote(kv_st.at[chip], kv_buf.at[0, :, c], kv_ss.at[0], kv_rs.at[0, c], sib))
    kv_send(3)
    q_block(5, xl)
    q_send(2)
    q_send(3)
    rows_mine = pl.ds(pl.multiple_of(128 * c, 128), 128)
    rows_sib = pl.ds(pl.multiple_of(128 * (1 - c), 128), 128)
    start(remote(q_st.at[chip, rows_sib], q_buf.at[0, c], q_ss.at[0, 0], q_rs.at[0, c], sib))
    for i in (4, 5, 6, 7):
        kv_send(i)
        q_send(i)

    q_buf[0, c] = q_st[chip, rows_mine]
    kv_buf[0, 0, c] = kv_st[chip, 0]
    kv_buf[0, 1, c] = kv_st[chip, 1]
    total[...] = jnp.zeros_like(total)
    sizes = [lens[0, u] for u in range(4)]
    starts = [0, sizes[0], sizes[0] + sizes[1], sizes[0] + sizes[1] + sizes[2]]

    def pick(pos, values):
        got = jnp.where(pos >= starts[1], values[1], values[0])
        got = jnp.where(pos >= starts[2], values[2], got)
        return jnp.where(pos >= starts[3], values[3], got)

    half_row = lax.broadcasted_iota(jnp.int32, (128, HEAD), 0) + 128 * c
    col = lax.broadcasted_iota(jnp.int32, (128, HEAD), 1)
    factor = 0.5 / math.sqrt(HEAD)
    for i in range(8):
        for core in range(2):
            first = order[0, 2 * comes[i] + core] * ROWS
            k_from[2 * i + core] = first
            pos = half_row + first
            q_pos[i, core] = pos
            q_low[i, core] = pick(pos, starts)

    def tile(q, k, v, first, low, high=None):
        half = jnp.dot(q, k, preferred_element_type=F32) * factor
        weight = half + half * jnp.tanh(half)
        parts = []
        for j in range(2):
            k_pos = col + (first + HEAD * j)
            seen = k_pos >= low
            if high is not None:
                seen = seen & (k_pos <= high)
            part = weight[:, HEAD * j : HEAD * (j + 1)]
            parts.append(jnp.where(seen, part, 0.0).astype(BF16))
        return jnp.dot(jnp.concatenate(parts, axis=1), v, preferred_element_type=F32)

    def alone(i, a):
        return tile(
            q_buf[i, a], key[i, a], kv_buf[i, 1, a], k_from[2 * i + a], q_low[i, a], q_pos[i, a]
        )

    def either(i, a, j, b):
        one, two = k_from[2 * i + a], k_from[2 * j + b]
        later = one > two
        value = tile(
            jnp.where(later, q_buf[i, a], q_buf[j, b]),
            jnp.where(later, key[j, b], key[i, a]),
            jnp.where(later, kv_buf[j, 1, b], kv_buf[i, 1, a]),
            jnp.minimum(one, two),
            jnp.where(later, q_low[i, a], q_low[j, b]),
        )
        return jnp.where(later, value, 0.0), jnp.where(later, 0.0, value)

    def within(i):
        one, two = alone(i, 0), alone(i, 1)
        more = either(i, 0, i, 1)
        total[i, 0] += one + more[0]
        total[i, 1] += two + more[1]

    def between(i, j):
        got = [[either(i, a, j, b) for b in range(2)] for a in range(2)]
        for a in range(2):
            total[i, a] += got[a][0][0] + got[a][1][0]
        for b in range(2):
            total[j, b] += got[0][b][1] + got[1][b][1]

    def turn_keys(i):
        for core in range(2):
            key[i, core] = kv_buf[i, 0, core].T

    def kv_wait(i, core):
        ref = kv_buf.at[i, :, core]
        remote(ref, ref, kv_ss.at[0], kv_rs.at[i, core], sib).wait_recv()

    def q_wait(i, core):
        ref = q_buf.at[i, core]
        remote(ref, ref, q_ss.at[0, 0], q_rs.at[i, core], sib).wait_recv()

    def finish(i):
        for core in range(2):
            size = pick(q_pos[i, core], sizes).astype(F32)
            att_st[i, core] = (total[i, core] / size).astype(BF16)
        if i == 0:
            start(remote(att_st.at[0, 1 - c], heads.at[me], a_ss.at[0, 0], a_rs.at[me], sib))
            heads[me] = att_st[0, c]
        else:
            for core in range(2):
                target = (dp, 2 * comes[i] + core)
                start(
                    remote(att_st.at[i, core], heads.at[me], a_ss.at[i, core], a_rs.at[me], target)
                )

    def kv_pass(i):
        kv_wait(i, c)
        ref = kv_buf.at[i, :, c]
        start(remote(ref, ref, kv_fs.at[i], kv_rs.at[i, c], sib))

    gate[:, pl.ds(0, 512)] = block(6)
    gate[:, pl.ds(512, 512)] = block(7)
    kv_wait(0, 1 - c)
    q_wait(0, 1 - c)
    turn_keys(0)
    within(0)
    ring(0, 1)
    steps = [(1, 0), (1, 1), (2, 0), (2, 1), (3, 0), (3, 1)]
    kv_pass(1)
    for i in range(1, 8):
        if i < 7:
            kv_pass(i + 1)
        kv_wait(i, 1 - c)
        q_wait(i, 0)
        q_wait(i, 1)
        turn_keys(i)
        within(i)
        if i < 7:

            def older(j, carry, i=i):
                between(i, j)
                return carry

            lax.fori_loop(0, i, older, 0)
            ring(*steps[i - 1])
    for j in (1, 2, 3, 4, 5, 6, 0):
        between(7, j)
        finish(j)
    finish(7)

    ids = neg_ids[...].astype(F32)
    ids = jnp.concatenate([ids, jnp.zeros((112, 128), F32)], axis=0).T.reshape(8, 2, 8, 128)
    ids = jnp.where(c == 0, ids[:, 0], ids[:, 1]).reshape(64, 128)
    for copy in loads:
        copy.wait()
    neg_wait(lax.rem(z + 4, 8))
    neg_wait(8 + lax.rem(z + 4, 8))
    for k in range(1, SLOTS):
        j = lax.rem(me + k, SLOTS)
        remote(heads.at[j], heads.at[j], n_xs, a_rs.at[j], sib).wait_recv()
    for core in range(2):
        rows = pl.ds(128 * core, 128)
        attended = jnp.concatenate([heads[2 * h + core] for h in range(HEADS)], axis=1)
        mixed[rows] = (norm(attended.astype(F32)) * gate[rows].astype(F32)).astype(BF16)
    vec = events[...].astype(F32) + jnp.dot(mixed[...], w_out[...], preferred_element_type=F32)
    users[0] = vec.astype(BF16)
    u_copy = remote(users.at[0], users.at[1], u_sem.at[0], u_sem.at[1], sib)
    start(u_copy)
    scale = 1.0 / math.sqrt(WIDTH)
    pos_col = jnp.sum(users[0].astype(F32) * targets[...].astype(F32), axis=1, keepdims=True) * scale
    eye = lax.broadcasted_iota(jnp.int32, (ROWS, ROWS), 0) == lax.broadcasted_iota(
        jnp.int32, (ROWS, ROWS), 1
    )
    pos = jnp.sum(jnp.where(eye, pos_col, 0.0), axis=0, keepdims=True)

    def score(side, top):
        for d in range(0, SLOTS, 4):
            part = neg[pl.ds(d, 4)].reshape(ROWS, WIDTH)
            scores = (
                lax.dot_general(
                    part, users[side], (((1,), (1,)), ((), ())), preferred_element_type=F32
                )
                * scale
            )
            id_col = jnp.concatenate([ids[:, d + i : d + i + 1] for i in range(4)], axis=0)
            scores = jnp.where(id_col != wanted[side], scores, -jnp.inf)
            top = jnp.maximum(top, jnp.max(scores, axis=0, keepdims=True))
            logits[side, pl.ds(64 * d, ROWS)] = scores
        return top

    def weigh(side, top, whole):
        for d in range(4):
            rows = pl.ds(ROWS * d, ROWS)
            weight = jnp.exp(logits[side, rows] - top)
            logits[side, rows] = weight
            whole = whole + jnp.sum(weight, axis=0, keepdims=True)
        stats[2 * side : 2 * side + 1] = top
        stats[2 * side + 1 : 2 * side + 2] = whole

    top = score(0, pos)
    weigh(0, top, jnp.exp(pos - top))
    t_copy.wait_recv()
    u_copy.wait_recv()
    top = score(1, jnp.full((1, ROWS), -1e30, F32))
    weigh(1, top, jnp.zeros((1, ROWS), F32))
    s_copy = remote(stats, stats_sib, s_sem.at[0], s_sem.at[1], sib)
    start(s_copy)
    s_copy.wait_recv()
    for side in range(2):
        near_top, near_sum = stats[2 * side : 2 * side + 1], stats[2 * side + 1 : 2 * side + 2]
        far = 2 * (1 - side)
        far_top, far_sum = stats_sib[far : far + 1], stats_sib[far + 1 : far + 2]
        top = jnp.maximum(near_top, far_top)
        near, far = jnp.exp(near_top - top), jnp.exp(far_top - top)
        whole = near_sum * near + far_sum * far
        if side == 0:
            loss_out[...] = top + jnp.log(whole) - pos
        factor = near / whole
        for d in range(4):
            rows = pl.ds(ROWS * d, ROWS)
            prob[rows, pl.ds(ROWS * side, ROWS)] = (logits[side, rows] * factor).astype(BF16)

    def grad_block(n, a, b):
        rows = pl.ds(pl.multiple_of((a * 8 + 4 * b) * 64, 256), 256)
        sides = []
        for k in range(2):
            value = jnp.dot(
                prob[rows],
                users[:, :, pl.ds(512 * k + 256 * n, 256)].reshape(2 * ROWS, 256),
                preferred_element_type=F32,
            )
            sides.append(value.reshape(4, 2, 4, 8, 256))
        grad[n, a, pl.ds(4 * b, 4)] = jnp.concatenate(sides, axis=3).astype(BF16)

    def send_x(n, k):
        a, b = xs[k]
        start(
            remote(
                grad.at[n, a, pl.ds(0, 4), b], ra1.at[n, k], g_ss.at[n, k], g_rs.at[n, k], x_peers[k]
            )
        )

    def send_y(n, k, a):
        i = 3 + 2 * k + a
        start(
            remote(
                grad.at[n, a, pl.ds(4, 4), :, ys[k]],
                rb1.at[n, k, a],
                g_ss.at[n, i],
                g_rs.at[n, i],
                y_peers[k],
            )
        )

    for n in range(2):
        grad_block(n, 1 - xh, 0)
        send_x(n, 2)
        send_x(n, 1)
        grad_block(n, 0, 1)
        for k in (1, 0, 2):
            send_y(n, k, 0)
        grad_block(n, xh, 0)
        send_x(n, 0)
        grad_block(n, 1, 1)
        for k in (1, 0, 2):
            send_y(n, k, 1)

    def wide(ref):
        return ref[...].astype(F32)

    for n in range(2):
        for k in range(3):
            remote(ra1.at[n, k], ra1.at[n, k], g_ss.at[n, k], g_rs.at[n, k], sib).wait_recv()
        sa[n] = (
            wide(grad.at[n, xh, pl.ds(0, 4), xl]) + wide(ra1.at[n, 0]) + wide(ra1.at[n, 1]) + wide(ra1.at[n, 2])
        ).astype(BF16)
        for k in (1, 0, 2):
            start(
                remote(sa.at[n, :, ys[k]], ra2.at[n, k], h_ss.at[n, k], h_rs.at[n, k], y_peers[k])
            )
        for k in range(3):
            for a in range(2):
                ref = rb1.at[n, k, a]
                remote(ref, ref, g_ss.at[n, 0], g_rs.at[n, 3 + 2 * k + a], sib).wait_recv()
        sb[n] = (
            wide(grad.at[n, :, pl.ds(4, 4), :, y])
            + wide(rb1.at[n, 0])
            + wide(rb1.at[n, 1])
            + wide(rb1.at[n, 2])
        ).astype(BF16)
        for k in (2, 1, 0):
            a, b = xs[k]
            start(
                remote(
                    sb.at[n, a, :, b], rb2.at[n, k], h_ss.at[n, 3 + k], h_rs.at[n, 3 + k], x_peers[k]
                )
            )
    for n in range(2):
        for k in range(3):
            remote(ra2.at[n, k], ra2.at[n, k], h_ss.at[n, 0], h_rs.at[n, k], sib).wait_recv()
        tz[n, pl.ds(0, 4)] = (
            wide(sa.at[n, :, y]) + wide(ra2.at[n, 0]) + wide(ra2.at[n, 1]) + wide(ra2.at[n, 2])
        ).astype(BF16)
        for k in range(3):
            remote(rb2.at[n, k], rb2.at[n, k], h_ss.at[n, 0], h_rs.at[n, 3 + k], sib).wait_recv()
        tz[n, pl.ds(4, 4)] = (
            wide(sb.at[n, xh, :, xl]) + wide(rb2.at[n, 0]) + wide(rb2.at[n, 1]) + wide(rb2.at[n, 2])
        ).astype(BF16)
        for k in (3, 2, 4, 1, 5, 0, 6):
            start(remote(tz.at[n, zs[k]], rz.at[n, k], z_ss.at[n, k], z_rs.at[n, k], z_peers[k]))
    for n in range(2):
        result = tz[n, z].astype(F32)
        for k in range(7):
            remote(rz.at[n, k], rz.at[n, k], z_ss.at[n, 0], z_rs.at[n, k], sib).wait_recv()
            result = result + rz[n, k].astype(F32)
        result = result * scale
        grad_out[:, pl.ds(256 * n, 256)] = result[:8]
        grad_out[:, pl.ds(512 + 256 * n, 256)] = result[8:]
    for copy in sends:
        copy.wait_send()


def shards(events, w_in, w_out, targets, target_ids, lengths, block_order, negatives, neg_ids):
    any_space = pl.BlockSpec(memory_space=pl.ANY)
    vmem = pl.BlockSpec(memory_space=pltpu.VMEM)
    smem = pl.BlockSpec(memory_space=pltpu.SMEM)
    dma = pltpu.SemaphoreType.DMA
    loss, grad = pl.pallas_call(
        program_kernel,
        out_shape=(
            jax.ShapeDtypeStruct((1, ROWS), F32),
            jax.ShapeDtypeStruct((8, WIDTH), F32),
        ),
        in_specs=[vmem, any_space, vmem, smem, smem, any_space, vmem, any_space, vmem],
        out_specs=(vmem, vmem),
        scratch_shapes=[
            pltpu.VMEM((8, WIDTH, 512), BF16),
            pltpu.VMEM((ROWS, WIDTH), BF16),
            pltpu.VMEM((HEADS, 2, ROWS, HEAD), BF16),
            pltpu.VMEM((HEADS, ROWS, HEAD), BF16),
            pltpu.VMEM((8, 2, 2, ROWS, HEAD), BF16),
            pltpu.VMEM((8, 2, 128, HEAD), BF16),
            pltpu.VMEM((8, 2, HEAD, ROWS), BF16),
            pltpu.VMEM((8, 2, 128, HEAD), jnp.int32),
            pltpu.VMEM((8, 2, 128, HEAD), jnp.int32),
            pltpu.VMEM((8, 2, 128, HEAD), F32),
            pltpu.VMEM((8, 2, 128, HEAD), BF16),
            pltpu.SMEM((SLOTS,), jnp.int32),
            pltpu.VMEM((SLOTS, 128, HEAD), BF16),
            pltpu.VMEM((ROWS, WIDTH), BF16),
            pltpu.VMEM((ROWS, WIDTH), BF16),
            pltpu.VMEM((WIDTH, WIDTH), BF16),
            pltpu.VMEM((8, 2, 8, WIDTH), F32),
            pltpu.VMEM((SLOTS, 64, WIDTH), BF16),
            pltpu.VMEM((ROWS, WIDTH), BF16),
            pltpu.VMEM((2, ROWS, WIDTH), BF16),
            pltpu.VMEM((2, 1, ROWS), F32),
            pltpu.VMEM((8, ROWS), F32),
            pltpu.VMEM((8, ROWS), F32),
            pltpu.VMEM((2, 1024, ROWS), F32),
            pltpu.VMEM((1024, 2 * ROWS), BF16),
            pltpu.VMEM((2, 2, 8, 2, 4, 16, 256), BF16),
            pltpu.VMEM((2, 3, 4, 4, 16, 256), BF16),
            pltpu.VMEM((2, 3, 2, 4, 2, 16, 256), BF16),
            pltpu.VMEM((2, 4, 4, 16, 256), BF16),
            pltpu.VMEM((2, 2, 4, 2, 16, 256), BF16),
            pltpu.VMEM((2, 3, 4, 16, 256), BF16),
            pltpu.VMEM((2, 3, 4, 16, 256), BF16),
            pltpu.VMEM((2, 8, 16, 256), BF16),
            pltpu.VMEM((2, 7, 16, 256), BF16),
            dma((8,)),
            dma((2,)),
            dma((8,)),
            dma((8,)),
            dma((8, 2)),
            dma((8, 2)),
            dma((8, 2)),
            dma,
            dma((2, 7)),
            dma((SLOTS,)),
            dma((8, 2)),
            dma((SLOTS,)),
            dma((2,)),
            dma((2,)),
            dma((2,)),
            dma((2, 9)),
            dma((2, 9)),
            dma((2, 6)),
            dma((2, 6)),
            dma((2, 7)),
            dma((2, 7)),
        ],
        compiler_params=pltpu.CompilerParams(
            collective_id=1, has_side_effects=True, vmem_limit_bytes=VMEM_LIMIT
        ),
        name="program",
    )(
        events, w_in, negatives, lengths, block_order, targets, target_ids.reshape(1, ROWS), w_out,
        neg_ids.reshape(SLOTS, 128),
    )
    return (loss.reshape(ROWS), grad)


def solution(mesh):
    return jax.shard_map(
        shards,
        mesh=mesh,
        in_specs=(
            P(("dp", "ctx"), None),
            P(),
            P(),
            P(("dp", "ctx"), None),
            P(("dp", "ctx")),
            P("dp", None),
            P("dp", None),
            P("dp", None),
            P(),
        ),
        out_specs=(P(("dp", "ctx")), P(("dp", "ctx"), None)),
        check_vma=False,
    )
```

```python
import functools
import math

import jax
import jax.numpy as jnp
from jax import lax
from jax.experimental import pallas as pl
from jax.experimental.pallas import tpu as pltpu
from jax.sharding import PartitionSpec as P

MESH = pl.DeviceIdType.MESH
F32 = jnp.float32
BF16 = jnp.bfloat16
ROWS, WIDTH, HEADS, HEAD = 256, 1024, 8, 128
SLOTS = 16
VMEM_LIMIT = 56 * 2**20
PEERS = [(1, 0), (0, 1), (1, 1), (0, 3), (1, 3), (0, 2), (1, 2)]


def place():
    dp = lax.axis_index("dp")
    ctx = lax.axis_index("ctx")
    return dp // 8, dp % 8, ctx // 8, (ctx // 2) % 4, ctx % 2


def device(xh, z, xl, y, c):
    return (xh * 8 + z, xl * 8 + y * 2 + c)


def remote(src, dst, send, recv, dev):
    return pltpu.make_async_remote_copy(
        src_ref=src, dst_ref=dst, send_sem=send, recv_sem=recv, device_id=dev, device_id_type=MESH
    )


def greet(others):
    barrier = pltpu.get_barrier_semaphore()
    for other in others:
        pl.semaphore_signal(barrier, inc=1, device_id=other, device_id_type=MESH)
    return barrier, len(others)


def silu(values):
    half = values * 0.5
    return half + half * jnp.tanh(half)


def norm(values):
    center = values - jnp.mean(values, axis=-1, keepdims=True)
    spread = jnp.mean(center * center, axis=-1, keepdims=True)
    return center * lax.rsqrt(spread + 1e-05)


def program_kernel(
    events, w_in, neg_in, lens, order, targets_in, target_ids, w_out_in, neg_ids,
    loss_out, grad_out,
    w_buf, normed, kv_st, q_st, kv_buf, q_buf, key, q_pos, q_low, total, att_st, k_from,
    heads, gate, targets, w_out, neg_rows, neg, mixed, users, wanted, stats, stats_sib,
    logits, prob, grad, ta, tb, ra1, rb1, sa, sb, ra2, rb2, tz, rz,
    w_sem, loc_sem, kv_ss, kv_fs, kv_rs, q_ss, q_rs, n_xs, n_ss, n_rs, a_ss, a_rs,
    u_sem, t_sem, s_sem, g_ss, g_rs, h_ss, h_rs, z_ss, z_rs,
):
    xh, z, xl, y, c = place()
    dp = lax.axis_index("dp")
    me = lax.axis_index("ctx")
    chip = me // 2
    sib = (dp, chip * 2 + 1 - c)
    xs = [(xh, 1 - xl), (1 - xh, xl), (1 - xh, 1 - xl)]
    x_peers = [device(a, z, b, y, c) for a, b in xs]
    ys = [lax.rem(y + k, 4) for k in range(1, 4)]
    y_peers = [device(xh, z, xl, b, c) for b in ys]
    zs = [lax.rem(z + k, 8) for k in range(1, 8)]
    z_peers = [device(xh, b, xl, y, c) for b in zs]
    up, down, across = z_peers[0], z_peers[6], x_peers[1]
    goes = [chip] + [(xl + a) % 2 * 4 + lax.rem(y + b, 4) for a, b in PEERS]
    comes = [chip] + [(xl + a) % 2 * 4 + lax.rem(y + 4 - b, 4) for a, b in PEERS]

    barrier, count = greet(
        x_peers[1:] + z_peers + [(dp, lax.rem(me + k, SLOTS)) for k in range(1, SLOTS)]
    )
    far = (1 - xl) * 512
    near = xl * 512
    offsets = [3072 + far, 1024 + far, 2048 + far, 3072 + near, 1024 + near, 2048 + near, 0, 512]
    w_copies = [
        pltpu.make_async_copy(
            w_in.at[:, pl.ds(pl.multiple_of(off, 512), 512)], w_buf.at[i], w_sem.at[i]
        )
        for i, off in enumerate(offsets)
    ]
    for copy in w_copies:
        copy.start()
    loads = [
        pltpu.make_async_copy(w_out_in, w_out, loc_sem.at[0]),
        pltpu.make_async_copy(targets_in, targets, loc_sem.at[1]),
    ]
    for copy in loads:
        copy.start()
    neg_rows[...] = neg_in[...].astype(F32).reshape(8, 2, 8, WIDTH)
    neg[dp] = neg_rows[:, c].reshape(64, WIDTH).astype(BF16)
    normed[...] = norm(events[...].astype(F32)).astype(BF16)
    wanted[0] = target_ids[...].astype(F32)
    pl.semaphore_wait(barrier, count)

    sends = []

    def start(copy):
        copy.start()
        sends.append(copy)

    start(remote(neg.at[dp], neg.at[dp], n_xs, n_rs.at[dp], across))
    start(remote(neg.at[dp], neg.at[dp], n_ss.at[0, 0], n_rs.at[dp], up))
    start(remote(neg.at[dp], neg.at[dp], n_ss.at[1, 0], n_rs.at[dp], down))
    t_copy = remote(wanted.at[0], wanted.at[1], t_sem.at[0], t_sem.at[1], sib)
    start(t_copy)

    def neg_wait(index):
        remote(neg.at[index], neg.at[index], n_xs, n_rs.at[index], sib).wait_recv()

    def neg_pass(index, direction, i):
        target = up if direction == 0 else down
        start(remote(neg.at[index], neg.at[index], n_ss.at[direction, i], n_rs.at[index], target))

    def ring(s, side):
        mine = xh if side == 0 else 1 - xh
        ups = mine * 8 + lax.rem(z + 8 - s, 8)
        downs = mine * 8 + lax.rem(z + s, 8)
        neg_wait(ups)
        if s > 0:
            neg_wait(downs)
        if s < 3:
            neg_pass(ups, 0, 2 * s + side)
            neg_pass(downs, 1, 2 * s + side)
        elif side == 1:
            neg_pass(lax.rem(z + 5, 8), 0, 6)
            neg_pass(8 + lax.rem(z + 3, 8), 1, 6)

    def block(i):
        w_copies[i].wait()
        return silu(jnp.dot(normed[...], w_buf[i], preferred_element_type=F32)).astype(BF16)

    def kv_send(i):
        h = goes[i]
        start(remote(kv_st.at[h], kv_buf.at[i, :, c], kv_ss.at[i], kv_rs.at[i, c], (dp, 2 * h + c)))

    def q_send(i):
        h = goes[i]
        for core in range(2):
            part = q_st.at[h, pl.ds(128 * core, 128)]
            start(remote(part, q_buf.at[i, c], q_ss.at[i, core], q_rs.at[i, c], (dp, 2 * h + core)))

    def kv_block(i, part, side):
        value = block(i)
        for k in range(4):
            kv_st[4 * side + k, part] = value[:, 128 * k : 128 * (k + 1)]

    def q_block(i, side):
        value = block(i)
        for k in range(4):
            q_st[4 * side + k] = value[:, 128 * k : 128 * (k + 1)]

    kv_block(0, 0, 1 - xl)
    kv_block(1, 1, 1 - xl)
    kv_send(1)
    q_block(2, 1 - xl)
    q_send(1)
    kv_block(3, 0, xl)
    kv_block(4, 1, xl)
    kv_send(2)
    start(remote(kv_st.at[chip], kv_buf.at[0, :, c], kv_ss.at[0], kv_rs.at[0, c], sib))
    kv_send(3)
    q_block(5, xl)
    q_send(2)
    q_send(3)
    rows_mine = pl.ds(pl.multiple_of(128 * c, 128), 128)
    rows_sib = pl.ds(pl.multiple_of(128 * (1 - c), 128), 128)
    start(remote(q_st.at[chip, rows_sib], q_buf.at[0, c], q_ss.at[0, 0], q_rs.at[0, c], sib))
    for i in (4, 5, 6, 7):
        kv_send(i)
        q_send(i)

    q_buf[0, c] = q_st[chip, rows_mine]
    kv_buf[0, 0, c] = kv_st[chip, 0]
    kv_buf[0, 1, c] = kv_st[chip, 1]
    total[...] = jnp.zeros_like(total)
    sizes = [lens[0, u] for u in range(4)]
    starts = [0, sizes[0], sizes[0] + sizes[1], sizes[0] + sizes[1] + sizes[2]]

    def pick(pos, values):
        got = jnp.where(pos >= starts[1], values[1], values[0])
        got = jnp.where(pos >= starts[2], values[2], got)
        return jnp.where(pos >= starts[3], values[3], got)

    half_row = lax.broadcasted_iota(jnp.int32, (128, HEAD), 0) + 128 * c
    col = lax.broadcasted_iota(jnp.int32, (128, HEAD), 1)
    factor = 0.5 / math.sqrt(HEAD)
    for i in range(8):
        for core in range(2):
            first = order[0, 2 * comes[i] + core] * ROWS
            k_from[2 * i + core] = first
            pos = half_row + first
            q_pos[i, core] = pos
            q_low[i, core] = pick(pos, starts)

    def tile(q, k, v, first, low, high=None):
        half = jnp.dot(q, k, preferred_element_type=F32) * factor
        weight = half + half * jnp.tanh(half)
        parts = []
        for j in range(2):
            k_pos = col + (first + HEAD * j)
            seen = k_pos >= low
            if high is not None:
                seen = seen & (k_pos <= high)
            part = weight[:, HEAD * j : HEAD * (j + 1)]
            parts.append(jnp.where(seen, part, 0.0).astype(BF16))
        return jnp.dot(jnp.concatenate(parts, axis=1), v, preferred_element_type=F32)

    def alone(i, a):
        return tile(
            q_buf[i, a], key[i, a], kv_buf[i, 1, a], k_from[2 * i + a], q_low[i, a], q_pos[i, a]
        )

    def either(i, a, j, b):
        one, two = k_from[2 * i + a], k_from[2 * j + b]
        later = one > two
        value = tile(
            jnp.where(later, q_buf[i, a], q_buf[j, b]),
            jnp.where(later, key[j, b], key[i, a]),
            jnp.where(later, kv_buf[j, 1, b], kv_buf[i, 1, a]),
            jnp.minimum(one, two),
            jnp.where(later, q_low[i, a], q_low[j, b]),
        )
        return jnp.where(later, value, 0.0), jnp.where(later, 0.0, value)

    def within(i):
        one, two = alone(i, 0), alone(i, 1)
        more = either(i, 0, i, 1)
        total[i, 0] += one + more[0]
        total[i, 1] += two + more[1]

    def between(i, j):
        got = [[either(i, a, j, b) for b in range(2)] for a in range(2)]
        for a in range(2):
            total[i, a] += got[a][0][0] + got[a][1][0]
        for b in range(2):
            total[j, b] += got[0][b][1] + got[1][b][1]

    def turn_keys(i):
        for core in range(2):
            key[i, core] = kv_buf[i, 0, core].T

    def kv_wait(i, core):
        ref = kv_buf.at[i, :, core]
        remote(ref, ref, kv_ss.at[0], kv_rs.at[i, core], sib).wait_recv()

    def q_wait(i, core):
        ref = q_buf.at[i, core]
        remote(ref, ref, q_ss.at[0, 0], q_rs.at[i, core], sib).wait_recv()

    def finish(i):
        for core in range(2):
            size = pick(q_pos[i, core], sizes).astype(F32)
            att_st[i, core] = (total[i, core] / size).astype(BF16)
        if i == 0:
            start(remote(att_st.at[0, 1 - c], heads.at[me], a_ss.at[0, 0], a_rs.at[me], sib))
            heads[me] = att_st[0, c]
        else:
            for core in range(2):
                target = (dp, 2 * comes[i] + core)
                start(
                    remote(att_st.at[i, core], heads.at[me], a_ss.at[i, core], a_rs.at[me], target)
                )

    def kv_pass(i):
        kv_wait(i, c)
        ref = kv_buf.at[i, :, c]
        start(remote(ref, ref, kv_fs.at[i], kv_rs.at[i, c], sib))

    gate[:, pl.ds(0, 512)] = block(6)
    gate[:, pl.ds(512, 512)] = block(7)
    kv_wait(0, 1 - c)
    q_wait(0, 1 - c)
    turn_keys(0)
    within(0)
    ring(0, 1)
    steps = {1: [(1, 0)], 2: [(1, 1)], 4: [(2, 0)], 5: [(2, 1)], 6: []}
    kv_pass(1)
    for i in range(1, 8):
        if i < 7:
            kv_pass(i + 1)
        kv_wait(i, 1 - c)
        q_wait(i, 0)
        q_wait(i, 1)
        turn_keys(i)
        within(i)
        if i < 7:

            def older(j, carry, i=i):
                between(i, j)
                return carry

            lax.fori_loop(0, i, older, 0)
            for step in steps.get(i, []):
                ring(*step)
    for j in (1, 2, 3, 4, 5, 6, 0):
        between(7, j)
        finish(j)
    finish(7)
    ring(3, 0)
    ring(3, 1)

    ids = neg_ids[...].astype(F32)
    ids = jnp.concatenate([ids, jnp.zeros((112, 128), F32)], axis=0).T.reshape(8, 2, 8, 128)
    ids = jnp.where(c == 0, ids[:, 0], ids[:, 1]).reshape(64, 128)
    for copy in loads:
        copy.wait()
    for k in range(1, SLOTS):
        j = lax.rem(me + k, SLOTS)
        remote(heads.at[j], heads.at[j], n_xs, a_rs.at[j], sib).wait_recv()
    for core in range(2):
        rows = pl.ds(128 * core, 128)
        attended = jnp.concatenate([heads[2 * h + core] for h in range(HEADS)], axis=1)
        mixed[rows] = (norm(attended.astype(F32)) * gate[rows].astype(F32)).astype(BF16)
    vec = events[...].astype(F32) + jnp.dot(mixed[...], w_out[...], preferred_element_type=F32)
    users[0] = vec.astype(BF16)
    u_copy = remote(users.at[0], users.at[1], u_sem.at[0], u_sem.at[1], sib)
    start(u_copy)
    scale = 1.0 / math.sqrt(WIDTH)
    pos_col = jnp.sum(users[0].astype(F32) * targets[...].astype(F32), axis=1, keepdims=True) * scale
    eye = lax.broadcasted_iota(jnp.int32, (ROWS, ROWS), 0) == lax.broadcasted_iota(
        jnp.int32, (ROWS, ROWS), 1
    )
    pos = jnp.sum(jnp.where(eye, pos_col, 0.0), axis=0, keepdims=True)

    neg_wait(lax.rem(z + 4, 8))
    neg_wait(8 + lax.rem(z + 4, 8))

    def score(side, top):
        for d in range(0, SLOTS, 4):
            part = neg[pl.ds(d, 4)].reshape(ROWS, WIDTH)
            scores = (
                lax.dot_general(
                    part, users[side], (((1,), (1,)), ((), ())), preferred_element_type=F32
                )
                * scale
            )
            id_col = jnp.concatenate([ids[:, d + i : d + i + 1] for i in range(4)], axis=0)
            scores = jnp.where(id_col != wanted[side], scores, -jnp.inf)
            top = jnp.maximum(top, jnp.max(scores, axis=0, keepdims=True))
            logits[side, pl.ds(64 * d, ROWS)] = scores
        return top

    def weigh(side, top, whole):
        for d in range(4):
            rows = pl.ds(ROWS * d, ROWS)
            weight = jnp.exp(logits[side, rows] - top)
            logits[side, rows] = weight
            whole = whole + jnp.sum(weight, axis=0, keepdims=True)
        stats[2 * side : 2 * side + 1] = top
        stats[2 * side + 1 : 2 * side + 2] = whole

    top = score(0, pos)
    weigh(0, top, jnp.exp(pos - top))
    t_copy.wait_recv()
    u_copy.wait_recv()
    top = score(1, jnp.full((1, ROWS), -1e30, F32))
    weigh(1, top, jnp.zeros((1, ROWS), F32))
    s_copy = remote(stats, stats_sib, s_sem.at[0], s_sem.at[1], sib)
    start(s_copy)
    s_copy.wait_recv()
    for side in range(2):
        near_top, near_sum = stats[2 * side : 2 * side + 1], stats[2 * side + 1 : 2 * side + 2]
        far = 2 * (1 - side)
        far_top, far_sum = stats_sib[far : far + 1], stats_sib[far + 1 : far + 2]
        top = jnp.maximum(near_top, far_top)
        near, far = jnp.exp(near_top - top), jnp.exp(far_top - top)
        whole = near_sum * near + far_sum * far
        if side == 0:
            loss_out[...] = top + jnp.log(whole) - pos
        factor = near / whole
        for d in range(4):
            rows = pl.ds(ROWS * d, ROWS)
            prob[rows, pl.ds(ROWS * side, ROWS)] = (logits[side, rows] * factor).astype(BF16)

    def grad_block(n, a, b):
        rows = pl.ds(pl.multiple_of((a * 8 + 4 * b) * 64, 256), 256)
        sides = []
        for k in range(2):
            value = jnp.dot(
                prob[rows],
                users[:, :, pl.ds(512 * k + 256 * n, 256)].reshape(2 * ROWS, 256),
                preferred_element_type=F32,
            )
            sides.append(value.reshape(4, 2, 4, 8, 256))
        grad[n, a, pl.ds(4 * b, 4)] = jnp.concatenate(sides, axis=3).astype(BF16)

    ring_x = [lax.rem(2 * xh + xl + k, 4) for k in range(4)]
    ring_y = [lax.rem(y + k, 4) for k in range(4)]
    x_side = [device(p // 2, z, p % 2, y, c) for p in (ring_x[1], ring_x[3])]
    y_side = [device(xh, z, xl, p, c) for p in (ring_y[1], ring_y[3])]

    def part_a(n, k, half):
        p = ring_x[k]
        return grad.at[n, p // 2, pl.ds(2 * half, 2), p % 2]

    def part_b(n, k, half):
        return grad.at[n, half, pl.ds(4, 4), :, ring_y[k]]

    def first_a(n, way):
        start(
            remote(
                part_a(n, 2, way), ta.at[n, way], g_ss.at[n, way], g_rs.at[n, way], x_side[way]
            )
        )

    def plain_a(n, way):
        half = 1 - way
        start(
            remote(
                part_a(n, 1 + 2 * way, half),
                ra1.at[n, way, pl.ds(2 * half, 2)],
                g_ss.at[n, 2 + way],
                g_rs.at[n, 2 + way],
                x_side[way],
            )
        )

    def first_b(n, way):
        start(
            remote(
                part_b(n, 2, way), tb.at[n, way], g_ss.at[n, 6 + way], g_rs.at[n, 6 + way], y_side[way]
            )
        )

    def plain_b(n, way):
        half = 1 - way
        start(
            remote(
                part_b(n, 1 + 2 * way, half),
                rb1.at[n, way, half],
                g_ss.at[n, 8 + way],
                g_rs.at[n, 8 + way],
                y_side[way],
            )
        )

    for n in range(2):
        grad_block(n, 1 - xh, 0)
        first_a(n, 0)
        first_a(n, 1)
        grad_block(n, 0, 1)
        first_b(n, 0)
        grad_block(n, 1, 1)
        first_b(n, 1)
        plain_b(n, 0)
        plain_b(n, 1)
        grad_block(n, xh, 0)
        plain_a(n, 0)
        plain_a(n, 1)

    def wide(ref):
        return ref[...].astype(F32)

    def arrive(ref, sem):
        remote(ref, ref, n_xs, sem, sib).wait_recv()

    for n in range(2):
        for way in range(2):
            arrive(ta.at[n, way], g_rs.at[n, way])
            ta[n, way] = (wide(ta.at[n, way]) + wide(part_a(n, 1 + 2 * way, way))).astype(BF16)
            start(
                remote(
                    ta.at[n, way],
                    ra1.at[n, way, pl.ds(2 * way, 2)],
                    g_ss.at[n, 4 + way],
                    g_rs.at[n, 4 + way],
                    x_side[way],
                )
            )
        for way in range(2):
            arrive(tb.at[n, way], g_rs.at[n, 6 + way])
            tb[n, way] = (wide(tb.at[n, way]) + wide(part_b(n, 1 + 2 * way, way))).astype(BF16)
            start(
                remote(
                    tb.at[n, way],
                    rb1.at[n, way, way],
                    g_ss.at[n, 10 + way],
                    g_rs.at[n, 10 + way],
                    y_side[way],
                )
            )
    for n in range(2):
        for way in range(2):
            arrive(ra1.at[n, way, pl.ds(2 - 2 * way, 2)], g_rs.at[n, 2 + way])
            arrive(ra1.at[n, way, pl.ds(2 * way, 2)], g_rs.at[n, 4 + way])
        sa[n] = (
            wide(grad.at[n, xh, pl.ds(0, 4), xl]) + wide(ra1.at[n, 0]) + wide(ra1.at[n, 1])
        ).astype(BF16)
        for k in (1, 0, 2):
            start(
                remote(sa.at[n, :, ys[k]], ra2.at[n, k], h_ss.at[n, k], h_rs.at[n, k], y_peers[k])
            )
        for way in range(2):
            arrive(rb1.at[n, way, 1 - way], g_rs.at[n, 8 + way])
            arrive(rb1.at[n, way, way], g_rs.at[n, 10 + way])
        sb[n] = (
            wide(grad.at[n, :, pl.ds(4, 4), :, y]) + wide(rb1.at[n, 0]) + wide(rb1.at[n, 1])
        ).astype(BF16)
        for k in (2, 1, 0):
            a, b = xs[k]
            start(
                remote(
                    sb.at[n, a, :, b], rb2.at[n, k], h_ss.at[n, 3 + k], h_rs.at[n, 3 + k], x_peers[k]
                )
            )
    for n in range(2):
        for k in range(3):
            remote(ra2.at[n, k], ra2.at[n, k], h_ss.at[n, 0], h_rs.at[n, k], sib).wait_recv()
        tz[n, pl.ds(0, 4)] = (
            wide(sa.at[n, :, y]) + wide(ra2.at[n, 0]) + wide(ra2.at[n, 1]) + wide(ra2.at[n, 2])
        ).astype(BF16)
        for k in range(3):
            remote(rb2.at[n, k], rb2.at[n, k], h_ss.at[n, 0], h_rs.at[n, 3 + k], sib).wait_recv()
        tz[n, pl.ds(4, 4)] = (
            wide(sb.at[n, xh, :, xl]) + wide(rb2.at[n, 0]) + wide(rb2.at[n, 1]) + wide(rb2.at[n, 2])
        ).astype(BF16)
        for k in (3, 2, 4, 1, 5, 0, 6):
            start(remote(tz.at[n, zs[k]], rz.at[n, k], z_ss.at[n, k], z_rs.at[n, k], z_peers[k]))
    for n in range(2):
        result = tz[n, z].astype(F32)
        for k in range(7):
            remote(rz.at[n, k], rz.at[n, k], z_ss.at[n, 0], z_rs.at[n, k], sib).wait_recv()
            result = result + rz[n, k].astype(F32)
        result = result * scale
        grad_out[:, pl.ds(256 * n, 256)] = result[:8]
        grad_out[:, pl.ds(512 + 256 * n, 256)] = result[8:]
    for copy in sends:
        copy.wait_send()


def hand_over_kernel(loss_in, grad_in, loss_out, grad_out):
    loss_out[...] = loss_in[...]
    grad_out[...] = grad_in[...]


def shards(events, w_in, w_out, targets, target_ids, lengths, block_order, negatives, neg_ids):
    any_space = pl.BlockSpec(memory_space=pl.ANY)
    vmem = pl.BlockSpec(memory_space=pltpu.VMEM)
    smem = pl.BlockSpec(memory_space=pltpu.SMEM)
    dma = pltpu.SemaphoreType.DMA
    loss, grad = pl.pallas_call(
        program_kernel,
        out_shape=(
            jax.ShapeDtypeStruct((1, ROWS), F32),
            jax.ShapeDtypeStruct((8, WIDTH), F32),
        ),
        in_specs=[vmem, any_space, vmem, smem, smem, any_space, vmem, any_space, vmem],
        out_specs=(vmem, vmem),
        scratch_shapes=[
            pltpu.VMEM((8, WIDTH, 512), BF16),
            pltpu.VMEM((ROWS, WIDTH), BF16),
            pltpu.VMEM((HEADS, 2, ROWS, HEAD), BF16),
            pltpu.VMEM((HEADS, ROWS, HEAD), BF16),
            pltpu.VMEM((8, 2, 2, ROWS, HEAD), BF16),
            pltpu.VMEM((8, 2, 128, HEAD), BF16),
            pltpu.VMEM((8, 2, HEAD, ROWS), BF16),
            pltpu.VMEM((8, 2, 128, HEAD), jnp.int32),
            pltpu.VMEM((8, 2, 128, HEAD), jnp.int32),
            pltpu.VMEM((8, 2, 128, HEAD), F32),
            pltpu.VMEM((8, 2, 128, HEAD), BF16),
            pltpu.SMEM((SLOTS,), jnp.int32),
            pltpu.VMEM((SLOTS, 128, HEAD), BF16),
            pltpu.VMEM((ROWS, WIDTH), BF16),
            pltpu.VMEM((ROWS, WIDTH), BF16),
            pltpu.VMEM((WIDTH, WIDTH), BF16),
            pltpu.VMEM((8, 2, 8, WIDTH), F32),
            pltpu.VMEM((SLOTS, 64, WIDTH), BF16),
            pltpu.VMEM((ROWS, WIDTH), BF16),
            pltpu.VMEM((2, ROWS, WIDTH), BF16),
            pltpu.VMEM((2, 1, ROWS), F32),
            pltpu.VMEM((8, ROWS), F32),
            pltpu.VMEM((8, ROWS), F32),
            pltpu.VMEM((2, 1024, ROWS), F32),
            pltpu.VMEM((1024, 2 * ROWS), BF16),
            pltpu.VMEM((2, 2, 8, 2, 4, 16, 256), BF16),
            pltpu.VMEM((2, 2, 2, 4, 16, 256), BF16),
            pltpu.VMEM((2, 2, 4, 2, 16, 256), BF16),
            pltpu.VMEM((2, 2, 4, 4, 16, 256), BF16),
            pltpu.VMEM((2, 2, 2, 4, 2, 16, 256), BF16),
            pltpu.VMEM((2, 4, 4, 16, 256), BF16),
            pltpu.VMEM((2, 2, 4, 2, 16, 256), BF16),
            pltpu.VMEM((2, 3, 4, 16, 256), BF16),
            pltpu.VMEM((2, 3, 4, 16, 256), BF16),
            pltpu.VMEM((2, 8, 16, 256), BF16),
            pltpu.VMEM((2, 7, 16, 256), BF16),
            dma((8,)),
            dma((2,)),
            dma((8,)),
            dma((8,)),
            dma((8, 2)),
            dma((8, 2)),
            dma((8, 2)),
            dma,
            dma((2, 7)),
            dma((SLOTS,)),
            dma((8, 2)),
            dma((SLOTS,)),
            dma((2,)),
            dma((2,)),
            dma((2,)),
            dma((2, 12)),
            dma((2, 12)),
            dma((2, 6)),
            dma((2, 6)),
            dma((2, 7)),
            dma((2, 7)),
        ],
        compiler_params=pltpu.CompilerParams(
            collective_id=1, has_side_effects=True, vmem_limit_bytes=VMEM_LIMIT
        ),
        name="program",
    )(
        events, w_in, negatives, lengths, block_order, targets, target_ids.reshape(1, ROWS), w_out,
        neg_ids.reshape(SLOTS, 128),
    )
    loss, grad = pl.pallas_call(
        hand_over_kernel,
        out_shape=(
            jax.ShapeDtypeStruct((1, ROWS), F32),
            jax.ShapeDtypeStruct((8, WIDTH), F32),
        ),
        in_specs=[vmem, vmem],
        out_specs=(vmem, vmem),
        name="hand_over",
    )(loss, grad)
    return (loss.reshape(ROWS), grad)


def solution(mesh):
    return jax.shard_map(
        shards,
        mesh=mesh,
        in_specs=(
            P(("dp", "ctx"), None),
            P(),
            P(),
            P(("dp", "ctx"), None),
            P(("dp", "ctx")),
            P("dp", None),
            P("dp", None),
            P("dp", None),
            P(),
        ),
        out_specs=(P(("dp", "ctx")), P(("dp", "ctx"), None)),
        check_vma=False,
    )
```

```python
import functools
import math

import jax
import jax.numpy as jnp
from jax import lax
from jax.experimental import pallas as pl
from jax.experimental.pallas import tpu as pltpu
from jax.sharding import PartitionSpec as P

MESH = pl.DeviceIdType.MESH
F32 = jnp.float32
BF16 = jnp.bfloat16
ROWS, WIDTH, HEADS, HEAD = 256, 1024, 8, 128
SLOTS = 16
VMEM_LIMIT = 56 * 2**20
PEERS = [(1, 0), (0, 1), (1, 1), (0, 3), (1, 3), (0, 2), (1, 2)]


def place():
    dp = lax.axis_index("dp")
    ctx = lax.axis_index("ctx")
    return dp // 8, dp % 8, ctx // 8, (ctx // 2) % 4, ctx % 2


def device(xh, z, xl, y, c):
    return (xh * 8 + z, xl * 8 + y * 2 + c)


def remote(src, dst, send, recv, dev):
    return pltpu.make_async_remote_copy(
        src_ref=src, dst_ref=dst, send_sem=send, recv_sem=recv, device_id=dev, device_id_type=MESH
    )


def greet(others):
    barrier = pltpu.get_barrier_semaphore()
    for other in others:
        pl.semaphore_signal(barrier, inc=1, device_id=other, device_id_type=MESH)
    return barrier, len(others)


def silu(values):
    half = values * 0.5
    return half + half * jnp.tanh(half)


def norm(values):
    center = values - jnp.mean(values, axis=-1, keepdims=True)
    spread = jnp.mean(center * center, axis=-1, keepdims=True)
    return center * lax.rsqrt(spread + 1e-05)


def program_kernel(
    events, w_in, neg_in, lens, order, targets_in, target_ids, w_out_in, neg_ids,
    loss_out, grad_out,
    w_buf, normed, kv_st, q_st, kv_buf, q_buf, key, q_pos, q_low, total, att_st, k_from,
    heads, gate, targets, w_out, neg_rows, neg, mixed, users, wanted, stats, stats_sib,
    logits, prob, grad, ta, tb, ra1, rb1, sa, sb, ra2, rb2, tz, rz,
    w_sem, loc_sem, kv_ss, kv_fs, kv_rs, q_ss, q_rs, n_xs, n_ss, n_rs, a_ss, a_rs,
    u_sem, t_sem, s_sem, g_ss, g_rs, h_ss, h_rs, z_ss, z_rs,
):
    xh, z, xl, y, c = place()
    dp = lax.axis_index("dp")
    me = lax.axis_index("ctx")
    chip = me // 2
    sib = (dp, chip * 2 + 1 - c)
    xs = [(xh, 1 - xl), (1 - xh, xl), (1 - xh, 1 - xl)]
    x_peers = [device(a, z, b, y, c) for a, b in xs]
    ys = [lax.rem(y + k, 4) for k in range(1, 4)]
    y_peers = [device(xh, z, xl, b, c) for b in ys]
    zs = [lax.rem(z + k, 8) for k in range(1, 8)]
    z_peers = [device(xh, b, xl, y, c) for b in zs]
    up, down, across = z_peers[0], z_peers[6], x_peers[1]
    goes = [chip] + [(xl + a) % 2 * 4 + lax.rem(y + b, 4) for a, b in PEERS]
    comes = [chip] + [(xl + a) % 2 * 4 + lax.rem(y + 4 - b, 4) for a, b in PEERS]

    far = (1 - xl) * 512
    near = xl * 512
    offsets = [3072 + far, 1024 + far, 2048 + far, 3072 + near, 1024 + near, 2048 + near, 0, 512]
    w_copies = [
        pltpu.make_async_copy(
            w_in.at[:, pl.ds(pl.multiple_of(off, 512), 512)], w_buf.at[i], w_sem.at[i]
        )
        for i, off in enumerate(offsets)
    ]
    for copy in w_copies:
        copy.start()
    barrier, count = greet(
        x_peers[1:] + z_peers + [(dp, lax.rem(me + k, SLOTS)) for k in range(1, SLOTS)]
    )
    loads = [
        pltpu.make_async_copy(w_out_in, w_out, loc_sem.at[0]),
        pltpu.make_async_copy(targets_in, targets, loc_sem.at[1]),
    ]
    for copy in loads:
        copy.start()
    normed[...] = norm(events[...].astype(F32)).astype(BF16)
    neg_rows[...] = neg_in[...].astype(F32).reshape(8, 2, 8, WIDTH)
    neg[dp] = neg_rows[:, c].reshape(64, WIDTH).astype(BF16)
    wanted[0] = target_ids[...].astype(F32)
    pl.semaphore_wait(barrier, count)

    sends = []

    def start(copy):
        copy.start()
        sends.append(copy)

    start(remote(neg.at[dp], neg.at[dp], n_xs, n_rs.at[dp], across))
    start(remote(neg.at[dp], neg.at[dp], n_ss.at[0, 0], n_rs.at[dp], up))
    start(remote(neg.at[dp], neg.at[dp], n_ss.at[1, 0], n_rs.at[dp], down))
    t_copy = remote(wanted.at[0], wanted.at[1], t_sem.at[0], t_sem.at[1], sib)
    start(t_copy)

    def neg_wait(index):
        remote(neg.at[index], neg.at[index], n_xs, n_rs.at[index], sib).wait_recv()

    def neg_pass(index, direction, i):
        target = up if direction == 0 else down
        start(remote(neg.at[index], neg.at[index], n_ss.at[direction, i], n_rs.at[index], target))

    def ring(s, side):
        mine = xh if side == 0 else 1 - xh
        ups = mine * 8 + lax.rem(z + 8 - s, 8)
        downs = mine * 8 + lax.rem(z + s, 8)
        neg_wait(ups)
        if s > 0:
            neg_wait(downs)
        if s < 3:
            neg_pass(ups, 0, 2 * s + side)
            neg_pass(downs, 1, 2 * s + side)
        elif side == 1:
            neg_pass(lax.rem(z + 5, 8), 0, 6)
            neg_pass(8 + lax.rem(z + 3, 8), 1, 6)

    def block(i):
        w_copies[i].wait()
        return silu(jnp.dot(normed[...], w_buf[i], preferred_element_type=F32)).astype(BF16)

    def kv_send(i):
        h = goes[i]
        start(remote(kv_st.at[h], kv_buf.at[i, :, c], kv_ss.at[i], kv_rs.at[i, c], (dp, 2 * h + c)))

    def q_send(i):
        h = goes[i]
        for core in range(2):
            part = q_st.at[h, pl.ds(128 * core, 128)]
            start(remote(part, q_buf.at[i, c], q_ss.at[i, core], q_rs.at[i, c], (dp, 2 * h + core)))

    def kv_block(i, part, side):
        value = block(i)
        for k in range(4):
            kv_st[4 * side + k, part] = value[:, 128 * k : 128 * (k + 1)]

    def q_block(i, side):
        value = block(i)
        for k in range(4):
            q_st[4 * side + k] = value[:, 128 * k : 128 * (k + 1)]

    kv_block(0, 0, 1 - xl)
    kv_block(1, 1, 1 - xl)
    kv_send(1)
    q_block(2, 1 - xl)
    q_send(1)
    kv_block(3, 0, xl)
    kv_block(4, 1, xl)
    kv_send(2)
    start(remote(kv_st.at[chip], kv_buf.at[0, :, c], kv_ss.at[0], kv_rs.at[0, c], sib))
    kv_send(3)
    q_block(5, xl)
    q_send(2)
    q_send(3)
    rows_mine = pl.ds(pl.multiple_of(128 * c, 128), 128)
    rows_sib = pl.ds(pl.multiple_of(128 * (1 - c), 128), 128)
    start(remote(q_st.at[chip, rows_sib], q_buf.at[0, c], q_ss.at[0, 0], q_rs.at[0, c], sib))
    for i in (4, 5, 6, 7):
        kv_send(i)
        q_send(i)

    q_buf[0, c] = q_st[chip, rows_mine]
    kv_buf[0, 0, c] = kv_st[chip, 0]
    kv_buf[0, 1, c] = kv_st[chip, 1]
    total[...] = jnp.zeros_like(total)
    sizes = [lens[0, u] for u in range(4)]
    starts = [0, sizes[0], sizes[0] + sizes[1], sizes[0] + sizes[1] + sizes[2]]

    def pick(pos, values):
        got = jnp.where(pos >= starts[1], values[1], values[0])
        got = jnp.where(pos >= starts[2], values[2], got)
        return jnp.where(pos >= starts[3], values[3], got)

    half_row = lax.broadcasted_iota(jnp.int32, (128, HEAD), 0) + 128 * c
    col = lax.broadcasted_iota(jnp.int32, (128, HEAD), 1)
    factor = 0.5 / math.sqrt(HEAD)
    for i in range(8):
        for core in range(2):
            first = order[0, 2 * comes[i] + core] * ROWS
            k_from[2 * i + core] = first
            pos = half_row + first
            q_pos[i, core] = pos
            q_low[i, core] = pick(pos, starts)

    def tile(q, k, v, first, low, high=None):
        half = jnp.dot(q, k, preferred_element_type=F32) * factor
        weight = half + half * jnp.tanh(half)
        parts = []
        for j in range(2):
            k_pos = col + (first + HEAD * j)
            seen = k_pos >= low
            if high is not None:
                seen = seen & (k_pos <= high)
            part = weight[:, HEAD * j : HEAD * (j + 1)]
            parts.append(jnp.where(seen, part, 0.0).astype(BF16))
        return jnp.dot(jnp.concatenate(parts, axis=1), v, preferred_element_type=F32)

    def alone(i, a):
        return tile(
            q_buf[i, a], key[i, a], kv_buf[i, 1, a], k_from[2 * i + a], q_low[i, a], q_pos[i, a]
        )

    def either(i, a, j, b):
        one, two = k_from[2 * i + a], k_from[2 * j + b]
        later = one > two
        value = tile(
            jnp.where(later, q_buf[i, a], q_buf[j, b]),
            jnp.where(later, key[j, b], key[i, a]),
            jnp.where(later, kv_buf[j, 1, b], kv_buf[i, 1, a]),
            jnp.minimum(one, two),
            jnp.where(later, q_low[i, a], q_low[j, b]),
        )
        return jnp.where(later, value, 0.0), jnp.where(later, 0.0, value)

    def within(i):
        one, two = alone(i, 0), alone(i, 1)
        more = either(i, 0, i, 1)
        total[i, 0] += one + more[0]
        total[i, 1] += two + more[1]

    def between(i, j):
        got = [[either(i, a, j, b) for b in range(2)] for a in range(2)]
        for a in range(2):
            total[i, a] += got[a][0][0] + got[a][1][0]
        for b in range(2):
            total[j, b] += got[0][b][1] + got[1][b][1]

    def turn_keys(i):
        for core in range(2):
            key[i, core] = kv_buf[i, 0, core].T

    def kv_wait(i, core):
        ref = kv_buf.at[i, :, core]
        remote(ref, ref, kv_ss.at[0], kv_rs.at[i, core], sib).wait_recv()

    def q_wait(i, core):
        ref = q_buf.at[i, core]
        remote(ref, ref, q_ss.at[0, 0], q_rs.at[i, core], sib).wait_recv()

    def finish(i):
        for core in range(2):
            size = pick(q_pos[i, core], sizes).astype(F32)
            att_st[i, core] = (total[i, core] / size).astype(BF16)
        if i == 0:
            start(remote(att_st.at[0, 1 - c], heads.at[me], a_ss.at[0, 0], a_rs.at[me], sib))
            heads[me] = att_st[0, c]
        else:
            for core in range(2):
                target = (dp, 2 * comes[i] + core)
                start(
                    remote(att_st.at[i, core], heads.at[me], a_ss.at[i, core], a_rs.at[me], target)
                )

    def kv_pass(i):
        kv_wait(i, c)
        ref = kv_buf.at[i, :, c]
        start(remote(ref, ref, kv_fs.at[i], kv_rs.at[i, c], sib))

    gate[:, pl.ds(0, 512)] = block(6)
    gate[:, pl.ds(512, 512)] = block(7)
    kv_wait(0, 1 - c)
    q_wait(0, 1 - c)
    turn_keys(0)
    within(0)
    ring(0, 1)
    steps = {1: [(1, 0)], 2: [(1, 1)], 4: [(2, 0)], 5: [(2, 1)], 6: []}
    kv_pass(1)
    for i in range(1, 8):
        if i < 7:
            kv_pass(i + 1)
        kv_wait(i, 1 - c)
        q_wait(i, 0)
        q_wait(i, 1)
        turn_keys(i)
        within(i)
        if i < 7:

            def older(j, carry, i=i):
                between(i, j)
                return carry

            lax.fori_loop(0, i, older, 0)
            for step in steps.get(i, []):
                ring(*step)
    for j in (1, 2, 3, 4, 5, 6, 0):
        between(7, j)
        finish(j)
    finish(7)
    ring(3, 0)
    ring(3, 1)

    ids = neg_ids[...].astype(F32)
    ids = jnp.concatenate([ids, jnp.zeros((112, 128), F32)], axis=0).T.reshape(8, 2, 8, 128)
    ids = jnp.where(c == 0, ids[:, 0], ids[:, 1]).reshape(64, 128)
    for copy in loads:
        copy.wait()
    for k in range(1, SLOTS):
        j = lax.rem(me + k, SLOTS)
        remote(heads.at[j], heads.at[j], n_xs, a_rs.at[j], sib).wait_recv()
    for core in range(2):
        rows = pl.ds(128 * core, 128)
        attended = jnp.concatenate([heads[2 * h + core] for h in range(HEADS)], axis=1)
        mixed[rows] = (norm(attended.astype(F32)) * gate[rows].astype(F32)).astype(BF16)
    vec = events[...].astype(F32) + jnp.dot(mixed[...], w_out[...], preferred_element_type=F32)
    users[0] = vec.astype(BF16)
    u_copy = remote(users.at[0], users.at[1], u_sem.at[0], u_sem.at[1], sib)
    start(u_copy)
    scale = 1.0 / math.sqrt(WIDTH)
    pos_col = jnp.sum(users[0].astype(F32) * targets[...].astype(F32), axis=1, keepdims=True) * scale
    eye = lax.broadcasted_iota(jnp.int32, (ROWS, ROWS), 0) == lax.broadcasted_iota(
        jnp.int32, (ROWS, ROWS), 1
    )
    pos = jnp.sum(jnp.where(eye, pos_col, 0.0), axis=0, keepdims=True)

    neg_wait(lax.rem(z + 4, 8))
    neg_wait(8 + lax.rem(z + 4, 8))

    def score(side, top):
        for d in range(0, SLOTS, 4):
            part = neg[pl.ds(d, 4)].reshape(ROWS, WIDTH)
            scores = (
                lax.dot_general(
                    part, users[side], (((1,), (1,)), ((), ())), preferred_element_type=F32
                )
                * scale
            )
            id_col = jnp.concatenate([ids[:, d + i : d + i + 1] for i in range(4)], axis=0)
            scores = jnp.where(id_col != wanted[side], scores, -jnp.inf)
            top = jnp.maximum(top, jnp.max(scores, axis=0, keepdims=True))
            logits[side, pl.ds(64 * d, ROWS)] = scores
        return top

    def weigh(side, top, whole):
        for d in range(4):
            rows = pl.ds(ROWS * d, ROWS)
            weight = jnp.exp(logits[side, rows] - top)
            logits[side, rows] = weight
            whole = whole + jnp.sum(weight, axis=0, keepdims=True)
        stats[side, 0:1] = top
        stats[side, 1:2] = whole
        copy = remote(
            stats.at[side], stats_sib.at[1 - side], s_sem.at[0, side], s_sem.at[1, side], sib
        )
        start(copy)
        return copy

    top = score(0, pos)
    one = weigh(0, top, jnp.exp(pos - top))
    t_copy.wait_recv()
    u_copy.wait_recv()
    top = score(1, jnp.full((1, ROWS), -1e30, F32))
    two = weigh(1, top, jnp.zeros((1, ROWS), F32))
    for side, copy in ((1, one), (0, two)):
        copy.wait_recv()
        near_top, near_sum = stats[side, 0:1], stats[side, 1:2]
        far_top, far_sum = stats_sib[side, 0:1], stats_sib[side, 1:2]
        top = jnp.maximum(near_top, far_top)
        near, far = jnp.exp(near_top - top), jnp.exp(far_top - top)
        whole = near_sum * near + far_sum * far
        if side == 0:
            loss_out[...] = top + jnp.log(whole) - pos
        factor = near / whole
        for d in range(4):
            rows = pl.ds(ROWS * d, ROWS)
            prob[rows, pl.ds(ROWS * side, ROWS)] = (logits[side, rows] * factor).astype(BF16)

    def grad_block(n, a, b):
        rows = pl.ds(pl.multiple_of((a * 8 + 4 * b) * 64, 256), 256)
        sides = []
        for k in range(2):
            value = jnp.dot(
                prob[rows],
                users[:, :, pl.ds(512 * k + 256 * n, 256)].reshape(2 * ROWS, 256),
                preferred_element_type=F32,
            )
            sides.append(value.reshape(4, 2, 4, 8, 256))
        grad[n, a, pl.ds(4 * b, 4)] = jnp.concatenate(sides, axis=3).astype(BF16)

    ring_x = [lax.rem(2 * xh + xl + k, 4) for k in range(4)]
    ring_y = [lax.rem(y + k, 4) for k in range(4)]
    x_side = [device(p // 2, z, p % 2, y, c) for p in (ring_x[1], ring_x[3])]
    y_side = [device(xh, z, xl, p, c) for p in (ring_y[1], ring_y[3])]

    def part_a(n, k, half):
        p = ring_x[k]
        return grad.at[n, p // 2, pl.ds(2 * half, 2), p % 2]

    def part_b(n, k, half):
        return grad.at[n, half, pl.ds(4, 4), :, ring_y[k]]

    def first_a(n, way):
        start(
            remote(
                part_a(n, 2, way), ta.at[n, way], g_ss.at[n, way], g_rs.at[n, way], x_side[way]
            )
        )

    def plain_a(n, way):
        half = 1 - way
        start(
            remote(
                part_a(n, 1 + 2 * way, half),
                ra1.at[n, way, pl.ds(2 * half, 2)],
                g_ss.at[n, 2 + way],
                g_rs.at[n, 2 + way],
                x_side[way],
            )
        )

    def first_b(n, way):
        start(
            remote(
                part_b(n, 2, way), tb.at[n, way], g_ss.at[n, 6 + way], g_rs.at[n, 6 + way], y_side[way]
            )
        )

    def plain_b(n, way):
        half = 1 - way
        start(
            remote(
                part_b(n, 1 + 2 * way, half),
                rb1.at[n, way, half],
                g_ss.at[n, 8 + way],
                g_rs.at[n, 8 + way],
                y_side[way],
            )
        )

    for n in range(2):
        grad_block(n, 1 - xh, 0)
        first_a(n, 0)
        first_a(n, 1)
        grad_block(n, 0, 1)
        first_b(n, 0)
        grad_block(n, 1, 1)
        first_b(n, 1)
        plain_b(n, 0)
        plain_b(n, 1)
        grad_block(n, xh, 0)
        plain_a(n, 0)
        plain_a(n, 1)

    def wide(ref):
        return ref[...].astype(F32)

    def arrive(ref, sem):
        remote(ref, ref, n_xs, sem, sib).wait_recv()

    def drain(keep):
        while len(sends) > keep:
            sends.pop(0).wait_send()

    drain(16)

    for n in range(2):
        for way in range(2):
            arrive(ta.at[n, way], g_rs.at[n, way])
            ta[n, way] = (wide(ta.at[n, way]) + wide(part_a(n, 1 + 2 * way, way))).astype(BF16)
            start(
                remote(
                    ta.at[n, way],
                    ra1.at[n, way, pl.ds(2 * way, 2)],
                    g_ss.at[n, 4 + way],
                    g_rs.at[n, 4 + way],
                    x_side[way],
                )
            )
        for way in range(2):
            arrive(tb.at[n, way], g_rs.at[n, 6 + way])
            tb[n, way] = (wide(tb.at[n, way]) + wide(part_b(n, 1 + 2 * way, way))).astype(BF16)
            start(
                remote(
                    tb.at[n, way],
                    rb1.at[n, way, way],
                    g_ss.at[n, 10 + way],
                    g_rs.at[n, 10 + way],
                    y_side[way],
                )
            )
    for n in range(2):
        for way in range(2):
            arrive(ra1.at[n, way, pl.ds(2 - 2 * way, 2)], g_rs.at[n, 2 + way])
            arrive(ra1.at[n, way, pl.ds(2 * way, 2)], g_rs.at[n, 4 + way])
        sa[n] = (
            wide(grad.at[n, xh, pl.ds(0, 4), xl]) + wide(ra1.at[n, 0]) + wide(ra1.at[n, 1])
        ).astype(BF16)
        for k in (1, 0, 2):
            start(
                remote(sa.at[n, :, ys[k]], ra2.at[n, k], h_ss.at[n, k], h_rs.at[n, k], y_peers[k])
            )
        for way in range(2):
            arrive(rb1.at[n, way, 1 - way], g_rs.at[n, 8 + way])
            arrive(rb1.at[n, way, way], g_rs.at[n, 10 + way])
        sb[n] = (
            wide(grad.at[n, :, pl.ds(4, 4), :, y]) + wide(rb1.at[n, 0]) + wide(rb1.at[n, 1])
        ).astype(BF16)
        for k in (2, 1, 0):
            a, b = xs[k]
            start(
                remote(
                    sb.at[n, a, :, b], rb2.at[n, k], h_ss.at[n, 3 + k], h_rs.at[n, 3 + k], x_peers[k]
                )
            )
    for n in range(2):
        for k in range(3):
            remote(ra2.at[n, k], ra2.at[n, k], h_ss.at[n, 0], h_rs.at[n, k], sib).wait_recv()
        drain(12)
        tz[n, pl.ds(0, 4)] = (
            wide(sa.at[n, :, y]) + wide(ra2.at[n, 0]) + wide(ra2.at[n, 1]) + wide(ra2.at[n, 2])
        ).astype(BF16)
        for k in range(3):
            remote(rb2.at[n, k], rb2.at[n, k], h_ss.at[n, 0], h_rs.at[n, 3 + k], sib).wait_recv()
        tz[n, pl.ds(4, 4)] = (
            wide(sb.at[n, xh, :, xl]) + wide(rb2.at[n, 0]) + wide(rb2.at[n, 1]) + wide(rb2.at[n, 2])
        ).astype(BF16)
        for k in (3, 2, 4, 1, 5, 0, 6):
            start(remote(tz.at[n, zs[k]], rz.at[n, k], z_ss.at[n, k], z_rs.at[n, k], z_peers[k]))
    drain(14)
    for n in range(2):
        result = tz[n, z].astype(F32)
        for k in range(7):
            remote(rz.at[n, k], rz.at[n, k], z_ss.at[n, 0], z_rs.at[n, k], sib).wait_recv()
            result = result + rz[n, k].astype(F32)
        result = result * scale
        grad_out[:, pl.ds(256 * n, 256)] = result[:8]
        grad_out[:, pl.ds(512 + 256 * n, 256)] = result[8:]
    for copy in sends:
        copy.wait_send()


def hand_over_kernel(loss_in, grad_in, loss_out, grad_out):
    loss_out[...] = loss_in[...]
    grad_out[...] = grad_in[...]


def shards(events, w_in, w_out, targets, target_ids, lengths, block_order, negatives, neg_ids):
    any_space = pl.BlockSpec(memory_space=pl.ANY)
    vmem = pl.BlockSpec(memory_space=pltpu.VMEM)
    smem = pl.BlockSpec(memory_space=pltpu.SMEM)
    dma = pltpu.SemaphoreType.DMA
    loss, grad = pl.pallas_call(
        program_kernel,
        out_shape=(
            jax.ShapeDtypeStruct((1, ROWS), F32),
            jax.ShapeDtypeStruct((8, WIDTH), F32),
        ),
        in_specs=[vmem, any_space, vmem, smem, smem, any_space, vmem, any_space, vmem],
        out_specs=(vmem, vmem),
        scratch_shapes=[
            pltpu.VMEM((8, WIDTH, 512), BF16),
            pltpu.VMEM((ROWS, WIDTH), BF16),
            pltpu.VMEM((HEADS, 2, ROWS, HEAD), BF16),
            pltpu.VMEM((HEADS, ROWS, HEAD), BF16),
            pltpu.VMEM((8, 2, 2, ROWS, HEAD), BF16),
            pltpu.VMEM((8, 2, 128, HEAD), BF16),
            pltpu.VMEM((8, 2, HEAD, ROWS), BF16),
            pltpu.VMEM((8, 2, 128, HEAD), jnp.int32),
            pltpu.VMEM((8, 2, 128, HEAD), jnp.int32),
            pltpu.VMEM((8, 2, 128, HEAD), F32),
            pltpu.VMEM((8, 2, 128, HEAD), BF16),
            pltpu.SMEM((SLOTS,), jnp.int32),
            pltpu.VMEM((SLOTS, 128, HEAD), BF16),
            pltpu.VMEM((ROWS, WIDTH), BF16),
            pltpu.VMEM((ROWS, WIDTH), BF16),
            pltpu.VMEM((WIDTH, WIDTH), BF16),
            pltpu.VMEM((8, 2, 8, WIDTH), F32),
            pltpu.VMEM((SLOTS, 64, WIDTH), BF16),
            pltpu.VMEM((ROWS, WIDTH), BF16),
            pltpu.VMEM((2, ROWS, WIDTH), BF16),
            pltpu.VMEM((2, 1, ROWS), F32),
            pltpu.VMEM((2, 8, ROWS), F32),
            pltpu.VMEM((2, 8, ROWS), F32),
            pltpu.VMEM((2, 1024, ROWS), F32),
            pltpu.VMEM((1024, 2 * ROWS), BF16),
            pltpu.VMEM((2, 2, 8, 2, 4, 16, 256), BF16),
            pltpu.VMEM((2, 2, 2, 4, 16, 256), BF16),
            pltpu.VMEM((2, 2, 4, 2, 16, 256), BF16),
            pltpu.VMEM((2, 2, 4, 4, 16, 256), BF16),
            pltpu.VMEM((2, 2, 2, 4, 2, 16, 256), BF16),
            pltpu.VMEM((2, 4, 4, 16, 256), BF16),
            pltpu.VMEM((2, 2, 4, 2, 16, 256), BF16),
            pltpu.VMEM((2, 3, 4, 16, 256), BF16),
            pltpu.VMEM((2, 3, 4, 16, 256), BF16),
            pltpu.VMEM((2, 8, 16, 256), BF16),
            pltpu.VMEM((2, 7, 16, 256), BF16),
            dma((8,)),
            dma((2,)),
            dma((8,)),
            dma((8,)),
            dma((8, 2)),
            dma((8, 2)),
            dma((8, 2)),
            dma,
            dma((2, 7)),
            dma((SLOTS,)),
            dma((8, 2)),
            dma((SLOTS,)),
            dma((2,)),
            dma((2,)),
            dma((2, 2)),
            dma((2, 12)),
            dma((2, 12)),
            dma((2, 6)),
            dma((2, 6)),
            dma((2, 7)),
            dma((2, 7)),
        ],
        compiler_params=pltpu.CompilerParams(
            collective_id=1, has_side_effects=True, vmem_limit_bytes=VMEM_LIMIT
        ),
        name="program",
    )(
        events, w_in, negatives, lengths, block_order, targets, target_ids.reshape(1, ROWS), w_out,
        neg_ids.reshape(SLOTS, 128),
    )
    loss, grad = pl.pallas_call(
        hand_over_kernel,
        out_shape=(
            jax.ShapeDtypeStruct((1, ROWS), F32),
            jax.ShapeDtypeStruct((8, WIDTH), F32),
        ),
        in_specs=[vmem, vmem],
        out_specs=(vmem, vmem),
        name="hand_over",
    )(loss, grad)
    return (loss.reshape(ROWS), grad)


def solution(mesh):
    return jax.shard_map(
        shards,
        mesh=mesh,
        in_specs=(
            P(("dp", "ctx"), None),
            P(),
            P(),
            P(("dp", "ctx"), None),
            P(("dp", "ctx")),
            P("dp", None),
            P("dp", None),
            P("dp", None),
            P(),
        ),
        out_specs=(P(("dp", "ctx")), P(("dp", "ctx"), None)),
        check_vma=False,
    )
```
